32 devices in a mesh: expert: 8 (over z, x), hidden: 4 (over y, core).
Axes of the slice: x: 2, y: 2, z: 4, core: 2. Of those that a mesh axis runs over, the one named last changes fastest.
Arguments:
- tokens: bfloat16 [16384, 1024], P(('expert', 'hidden')), may hold values from -6 to 6
- dispatch_rows: int32 [32, 8, 96], P(('expert', 'hidden')), may hold values from 0 to 512, as said below
- w_in: bfloat16 [8, 2, 1024, 4096], P('expert', None, None, 'hidden'), may hold values from -0.1875 to 0.1875
- w_out: bfloat16 [8, 2, 4096, 1024], P('expert', None, 'hidden'), may hold values from -0.09375 to 0.09375
- b_in: float32 [8, 2, 4096], P('expert', None, 'hidden'), may hold values from -3 to 3
- b_out: float32 [8, 2, 1024], P('expert'), may hold values from -2 to 2
- ln_gain: float32 [8, 2, 1024], P('expert'), may hold values from 0.5 to 1.5
- ln_bias: float32 [8, 2, 1024], P('expert'), may hold values from -2 to 2
- centroid: float32 [8, 1024], P('expert'), may hold values from -0.1875 to 0.1875
- cotangent: bfloat16 [16384, 1024], P(('expert', 'hidden')), may hold values from -6 to 6
Outputs:
- mixed: bfloat16 [16384, 1024], P(('expert', 'hidden'))
- grad_tokens: float32 [16384, 1024], P(('expert', 'hidden'))
- grad_w_in: float32 [8, 2, 1024, 4096], P('expert', None, None, 'hidden')
- grad_w_out: float32 [8, 2, 4096, 1024], P('expert', None, 'hidden')
- grad_b_in: float32 [8, 2, 4096], P('expert', None, 'hidden')
- grad_b_out: float32 [8, 2, 1024], P('expert')
- grad_gain: float32 [8, 2, 1024], P('expert')
- grad_ln_bias: float32 [8, 2, 1024], P('expert')
- grad_centroid: float32 [8, 1024], P('expert')
The draws below stay inside these ranges and needn't reach their ends.
Inputs may be any that keep to these rules, and one draw needn't show every extreme that they name: `dispatch_rows`: entry [s, e, c] names a token of device s that goes to expert e; the filled slots of a block come first, every token of a device stands in exactly one slot, and 512 marks an empty slot. A device fills at most 96 slots of one expert, some device fills all 96, and every expert receives the same number of tokens in all.
All inputs are finite; a program needn't handle non-finite values.
Results may differ from the reference program's by a relative error of at most 0.0067.
Values may be sent and summed in bfloat16 or wider, within the bound.
A program may use at most 256 MiB of HBM per device.

```python
import jax
import jax.numpy as jnp
from jax import lax

D = 1024
FF = 4096
SUBLAYERS = 2
TOK_DEV = 512
EXPERTS = 8
SOURCES = 32
TOKENS = 16384
CAP = 96


def draw_dispatch_rows(key, part):
    key = jax.random.fold_in(key, 17)
    key_pair, key_order, key_shift, key_tokens = jax.random.split(key, 4)
    mean_load = TOK_DEV // EXPERTS
    spread = CAP - mean_load
    offsets = jax.random.randint(key_pair, (EXPERTS // 2,), 0, spread + 1)
    offsets = offsets.at[0].set(0)
    loads = jnp.concatenate([CAP - offsets, 2 * mean_load - CAP + offsets])
    loads = loads[jax.random.permutation(key_order, EXPERTS)]
    shifts = jax.random.permutation(key_shift, EXPERTS)
    source_shift = jnp.tile(shifts, SOURCES // EXPERTS)
    column = (jnp.arange(EXPERTS)[None, :] + source_shift[:, None]) % EXPERTS
    counts = loads[column]
    starts = jnp.cumsum(counts, axis=1) - counts
    orders = jax.vmap(lambda k: jax.random.permutation(k, TOK_DEV))(jax.random.split(key_tokens, SOURCES))
    slot = jnp.arange(CAP)
    where = jnp.minimum(starts[:, :, None] + slot, TOK_DEV - 1).reshape(SOURCES, EXPERTS * CAP)
    picked = jnp.take_along_axis(orders, where, axis=1).reshape(SOURCES, EXPERTS, CAP)
    return jnp.where(slot < counts[:, :, None], picked, TOK_DEV).astype(jnp.int32)


def block_levels(own_key, extent, cuts, low, largest):
    level = 1.0
    for dim, shards_of in cuts:
        draws = jax.random.uniform(jax.random.fold_in(jax.random.fold_in(own_key, 6), dim), (shards_of,), jnp.float32, low / len(cuts), largest / len(cuts))
        level = level * jnp.repeat(jnp.exp(draws), extent[dim] // shards_of).reshape((-1,) + (1,) * (len(extent) - 1 - dim))
    return level


def normal_values(own_key, extent, scale, reach, shards=(), kind=jnp.bfloat16):
    factor_of = block_levels(own_key, extent, shards, -0.22, 0.18) if shards else 1.0
    result = jax.random.normal(own_key, extent, jnp.float32) * scale * factor_of
    return jnp.minimum(jnp.maximum(result, -reach), reach).astype(kind)


def setup_inputs(seed: int = 0) -> dict:
    seeds = jax.random.split(jax.random.key(seed), 11)
    tokens = normal_values(seeds[0], (TOKENS, D), 1.0, 6.0, ((0, 32),))
    dispatch_rows = draw_dispatch_rows(jax.random.fold_in(seeds[10], 71), 0)
    w_in = normal_values(seeds[2], (EXPERTS, SUBLAYERS, D, FF), D ** -0.5, 0.1875, ((0, 8), (3, 4)))
    w_out = normal_values(seeds[3], (EXPERTS, SUBLAYERS, FF, D), FF ** -0.5, 0.09375, ((0, 8), (2, 4)))
    b_in = normal_values(seeds[4], (EXPERTS, SUBLAYERS, FF), 0.5, 3.0, ((0, 8), (2, 4)), jnp.float32)
    b_out = normal_values(seeds[5], (EXPERTS, SUBLAYERS, D), 0.3, 2.0, ((0, 8),), jnp.float32)
    ln_gain = jnp.clip(1.0 + 0.1 * jax.random.normal(seeds[6], (EXPERTS, SUBLAYERS, D), jnp.float32), 0.5, 1.5)
    ln_bias = normal_values(seeds[7], (EXPERTS, SUBLAYERS, D), 0.3, 2.0, ((0, 8),), jnp.float32)
    centroid = normal_values(seeds[8], (EXPERTS, D), D ** -0.5, 0.1875, ((0, 8),), jnp.float32)
    cotangent = normal_values(seeds[9], (TOKENS, D), 1.0, 6.0, ((0, 32),))
    return dict(tokens=tokens, dispatch_rows=dispatch_rows, w_in=w_in, w_out=w_out, b_in=b_in, b_out=b_out, ln_gain=ln_gain, ln_bias=ln_bias, centroid=centroid, cotangent=cotangent)


@jax.custom_vjp
def low(v):
    return lax.optimization_barrier(v.astype(jnp.bfloat16)).astype(jnp.float32)

@jax.custom_vjp
def low_back(v):
    return v

def low_keep(v):
    return (low(v), None)

def low_pass(kept, grad):
    return (grad,)

def back_keep(v):
    return (v, None)

def back_low(kept, grad):
    return (low(grad),)
low.defvjp(low_keep, low_pass)
low_back.defvjp(back_keep, back_low)
eps_norm = 1e-05

def normalize(value, gain, shift):
    mean = lax.optimization_barrier(jnp.mean(value, axis=-1, keepdims=True))
    centered = value - mean
    scale = lax.rsqrt(lax.optimization_barrier(jnp.mean(centered * centered, axis=-1, keepdims=True)) + eps_norm)
    return centered * scale * gain + shift

def product(left, right):
    return jnp.dot(left, right, precision=lax.Precision.HIGHEST, preferred_element_type=jnp.float32)

def expert_rows(rows, w_in, w_out, b_in, b_out, ln_gain, ln_bias, centroid):
    state = rows
    for layer in range(SUBLAYERS):
        normed = low(normalize(state, ln_gain[layer], ln_bias[layer]))
        before = low_back(product(normed, w_in[layer]) + b_in[layer])
        active = low(jax.nn.gelu(before))
        state = state + low_back(product(active, w_out[layer])) + b_out[layer]
    share = jax.nn.sigmoid(lax.optimization_barrier(jnp.sum(rows * centroid, axis=-1, keepdims=True)))
    return share * state + (1.0 - share) * rows

def reference(tokens, dispatch_rows, w_in, w_out, b_in, b_out, ln_gain, ln_bias, centroid, cotangent):
    slots = dispatch_rows.reshape(SOURCES, EXPERTS * CAP).astype(jnp.int32)

    def forward(tokens_f, w_in_f, w_out_f, b_in_f, b_out_f, gain_f, shift_f, centroid_f):
        by_source = tokens_f.reshape(SOURCES, TOK_DEV, D)
        padded = jnp.concatenate([by_source, jnp.zeros((SOURCES, 1, D), jnp.float32)], axis=1)
        picked = jax.vmap(lambda rows, where: rows[where])(padded, slots)
        per_expert = picked.reshape(SOURCES, EXPERTS, CAP, D).transpose(1, 0, 2, 3).reshape(EXPERTS, SOURCES * CAP, D)
        checked = jax.checkpoint(expert_rows)

        def one_expert(item):
            return checked(*item)
        outputs = lax.map(one_expert, (per_expert, w_in_f, w_out_f, b_in_f, b_out_f, gain_f, shift_f, centroid_f))
        back = outputs.reshape(EXPERTS, SOURCES, CAP, D).transpose(1, 0, 2, 3).reshape(SOURCES, EXPERTS * CAP, D)
        placed = jax.vmap(lambda where, values: jnp.zeros((TOK_DEV + 1, D), jnp.float32).at[where].set(values))(slots, back)
        return placed[:, :TOK_DEV].reshape(TOKENS, D)
    mixed, pullback = jax.vjp(forward, tokens.astype(jnp.float32), w_in.astype(jnp.float32), w_out.astype(jnp.float32), b_in, b_out, ln_gain, ln_bias, centroid)
    grads = pullback(cotangent.astype(jnp.float32))
    return (mixed.astype(jnp.bfloat16), grads[0], grads[1], grads[2], grads[3], grads[4], grads[5], grads[6], grads[7])
```

```python
import functools

import jax
import jax.numpy as jnp
from jax import lax
from jax.experimental import pallas as pl
from jax.experimental.pallas import tpu as pltpu
from jax.sharding import PartitionSpec as P

MESH = pl.DeviceIdType.MESH
SUBLAYERS = 2
EPS = 1e-05
F32 = jnp.float32
BF16 = jnp.bfloat16
CHUNK = 256


def dot(left, right):
    return jnp.dot(left, right, preferred_element_type=F32)


def dot_tn(left, right):
    return lax.dot_general(left, right, (((0,), (0,)), ((), ())), preferred_element_type=F32)


def dot_nt(left, right):
    return lax.dot_general(left, right, (((1,), (1,)), ((), ())), preferred_element_type=F32)


def row_window(chunk, blocks, cap, rows):
    low = (chunk * CHUNK) // cap
    high = min(blocks - 1, (chunk * CHUNK + CHUNK - 1 + cap * blocks - rows) // cap)
    return low, high + 1


def dispatch_kernel(
    experts, cap, slots, tok, cot, xc, gc, pos, xsend, gsend, csend, xs, gs, cs, xh, gh, ps, pr, fs, fr, hs, hr, ls
):
    me = lax.axis_index("expert")
    place = lax.axis_index("hidden")
    y = place // 2
    c = lax.rem(place, 2)
    over_y = lax.rem(place + 2, 4)
    over_c = place + 1 - 2 * c
    blocks, capp, half = xs.shape
    toks, width = tok.shape
    rows = xc.shape[0]
    chunks = rows // CHUNK

    barrier = pltpu.get_barrier_semaphore()

    def greet(i, carry):
        e = lax.rem(me + i // 2, experts)
        cc = lax.rem(i, 2)

        @pl.when(jnp.logical_or(i // 2 > 0, cc != c))
        def _():
            pl.semaphore_signal(barrier, 1, device_id=(e, 2 * y + cc), device_id_type=MESH)

        return carry

    lax.fori_loop(0, 2 * experts, greet, 0)
    pl.semaphore_signal(barrier, 1, device_id=(me, over_y), device_id_type=MESH)
    pl.semaphore_wait(barrier, 2 * experts)

    sends = (xsend, gsend, csend)
    lands = (xs, gs, cs)

    def rank(d, yy, cc):
        return d * 4 + yy * 2 + cc

    def plane(a, d, cc):
        target = lax.rem(me + experts - d, experts)
        src = csend.at[target] if a == 2 else sends[a].at[cc, target]
        return pltpu.make_async_remote_copy(
            src_ref=src,
            dst_ref=lands[a].at[rank(d, y, c)],
            send_sem=ps.at[a, d, cc],
            recv_sem=pr.at[a, d, c],
            device_id=(target, 2 * y + cc),
            device_id_type=MESH,
        )

    def landed(a, d, cc):
        ref = lands[a].at[rank(d, y, cc)]
        return pltpu.make_async_remote_copy(
            src_ref=ref,
            dst_ref=ref,
            send_sem=ps.at[a, d, cc],
            recv_sem=pr.at[a, d, cc],
            device_id=(me, over_y),
            device_id_type=MESH,
        )

    def forward(a, d, cc):
        ref = lands[a].at[rank(d, y, cc)]
        return pltpu.make_async_remote_copy(
            src_ref=ref,
            dst_ref=ref,
            send_sem=fs.at[a, d, cc],
            recv_sem=fr.at[a, d, cc],
            device_id=(me, over_y),
            device_id_type=MESH,
        )

    def forwarded(a, d, cc):
        ref = lands[a].at[rank(d, 1 - y, cc)]
        return pltpu.make_async_remote_copy(
            src_ref=ref,
            dst_ref=ref,
            send_sem=fs.at[a, d, cc],
            recv_sem=fr.at[a, d, cc],
            device_id=(me, over_y),
            device_id_type=MESH,
        )

    lane = lax.broadcasted_iota(jnp.int32, (capp, 128), 1)
    slot = lax.broadcasted_iota(jnp.int32, (capp, 128), 0)

    def pick(target, source):
        where = slots[target]
        hot = jnp.concatenate([jnp.where(where == lane + 128 * t, 1.0, 0.0).astype(BF16) for t in range(toks // 128)], axis=1)
        return dot(hot, source[...]).astype(BF16)

    def start_x(d, cc):
        plane(2, d, cc).start()
        plane(0, d, cc).start()

    def fill(a, target):
        block = pick(target, cot if a else tok)
        sends[a][0, target] = block[:, :half]
        sends[a][1, target] = block[:, half:]

    def fill_x(target):
        fill(0, target)
        load = jnp.sum(jnp.where(slots[target] < toks, 1.0, 0.0), axis=0, keepdims=True)
        csend[target] = jnp.broadcast_to(load, (16, 128)).astype(BF16)

    fill_x(me)
    start_x(0, 1 - c)
    xs[rank(0, y, c)] = xsend[c, me]
    cs[rank(0, y, c)] = csend[me]
    forward(2, 0, c).start()
    forward(0, 0, c).start()

    def send_x(d, carry):
        fill_x(lax.rem(me + experts - d, experts))
        start_x(d, 0)
        start_x(d, 1)
        return carry

    lax.fori_loop(1, experts, send_x, 0)

    fill(1, me)
    plane(1, 0, 1 - c).start()
    gs[rank(0, y, c)] = gsend[c, me]

    def send_g(d, carry):
        fill(1, lax.rem(me + experts - d, experts))
        plane(1, d, 0).start()
        plane(1, d, 1).start()
        return carry

    lax.fori_loop(1, experts, send_g, 0)

    def pass_on(a, d, cc):
        landed(a, d, cc).wait_recv()
        forward(a, d, cc).start()

    pass_on(2, 0, 1 - c)
    pass_on(0, 0, 1 - c)

    def pass_x(d, carry):
        for cc in range(2):
            pass_on(2, d, cc)
            pass_on(0, d, cc)
        return carry

    lax.fori_loop(1, experts, pass_x, 0)
    forward(1, 0, c).start()
    pass_on(1, 0, 1 - c)

    def pass_g(d, carry):
        for cc in range(2):
            pass_on(1, d, cc)
        return carry

    def await_counts(d, carry):
        for cc in range(2):
            forwarded(2, d, cc).wait_recv()
        return carry

    lax.fori_loop(0, experts, await_counts, 0)

    def place_block(r, start):
        load = cs[r][0:8, :].astype(F32)[0:1, :].astype(jnp.int32)
        pos[r] = jnp.where(slot < load, start + slot, -1)
        return start + load

    lax.fori_loop(0, blocks, place_block, jnp.zeros((1, 128), jnp.int32))

    def pack_out(a, k):
        held = gh if a else xh
        out = gc if a else xc
        spot = out.at[pl.ds(k * CHUNK, CHUNK), pl.ds(pl.multiple_of(c * half, 128), half)]
        return (
            pltpu.make_async_copy(held.at[k], spot, ls.at[a, k]),
            pltpu.make_async_remote_copy(
                src_ref=held.at[k],
                dst_ref=spot,
                send_sem=hs.at[a, k],
                recv_sem=hr.at[a, k],
                device_id=(me, over_c),
                device_id_type=MESH,
            ),
        )

    def pack_in(a, k):
        out = gc if a else xc
        spot = out.at[pl.ds(k * CHUNK, CHUNK), pl.ds(pl.multiple_of((1 - c) * half, 128), half)]
        return pltpu.make_async_remote_copy(
            src_ref=spot,
            dst_ref=spot,
            send_sem=hs.at[a, k],
            recv_sem=hr.at[a, k],
            device_id=(me, over_c),
            device_id_type=MESH,
        )

    def pack(a, k):
        low, high = row_window(k, blocks, cap, rows)
        count = (high - low) * capp
        where = pos[low:high].reshape(count, 128)
        number = lax.broadcasted_iota(jnp.int32, (count, 128), 1) + k * CHUNK
        hot = jnp.concatenate([jnp.where(where == number + 128 * t, 1.0, 0.0).astype(BF16) for t in range(CHUNK // 128)], axis=1)
        held = gh if a else xh
        held[k] = dot_tn(hot, lands[a][low:high].reshape(count, half)).astype(BF16)
        for copy in pack_out(a, k):
            copy.start()

    def await_forwarded(a, low, high):
        def body(d, carry):
            for cc in range(2):
                forwarded(a, d, cc).wait_recv()
            return carry

        lax.fori_loop(low, high, body, 0)

    for a in range(2):
        done = 0
        for k in range(chunks):
            if a == 0:
                lax.fori_loop(1 + (k * (experts - 1)) // chunks, 1 + ((k + 1) * (experts - 1)) // chunks, pass_g, 0)
            need = -(-row_window(k, blocks, cap, rows)[1] // 4)
            await_forwarded(a, done, need)
            done = need
            pack(a, k)

    for a in range(2):
        for k in range(chunks):
            keep, give = pack_out(a, k)
            keep.wait()
            give.wait_send()
            pack_in(a, k).wait_recv()

    def drain(d, carry):
        for a in range(3):
            for cc in range(2):
                forward(a, d, cc).wait_send()
        return carry

    lax.fori_loop(0, experts, drain, 0)
    for a in range(3):
        plane(a, 0, 1 - c).wait_send()

    def drain_plane(d, carry):
        for a in range(3):
            for cc in range(2):
                plane(a, d, cc).wait_send()
        return carry

    lax.fori_loop(1, experts, drain_plane, 0)


def dispatch(slots, tokens, cotangent, experts, places):
    cap = slots.shape[1]
    capp = -(-cap // 16) * 16
    toks, width = tokens.shape
    rows = toks * places
    blocks = experts * places
    half = width // 2
    padded = jnp.pad(slots, ((0, 0), (0, capp - cap)), constant_values=toks)
    spread = jnp.broadcast_to(padded[:, :, None], (experts, capp, 128))
    chunks = rows // CHUNK
    vmem = pl.BlockSpec(memory_space=pltpu.VMEM)
    hbm = pl.BlockSpec(memory_space=pl.ANY)
    dma = pltpu.SemaphoreType.DMA
    return pl.pallas_call(
        functools.partial(dispatch_kernel, experts, cap),
        out_shape=(
            jax.ShapeDtypeStruct((rows, width), BF16),
            jax.ShapeDtypeStruct((rows, width), BF16),
            jax.ShapeDtypeStruct((blocks, capp, 128), jnp.int32),
        ),
        in_specs=[vmem, vmem, vmem],
        out_specs=(hbm, hbm, vmem),
        scratch_shapes=[
            pltpu.VMEM((2, experts, capp, half), BF16),
            pltpu.VMEM((2, experts, capp, half), BF16),
            pltpu.VMEM((experts, 16, 128), BF16),
            pltpu.VMEM((blocks, capp, half), BF16),
            pltpu.VMEM((blocks, capp, half), BF16),
            pltpu.VMEM((blocks, 16, 128), BF16),
            pltpu.VMEM((chunks, CHUNK, half), BF16),
            pltpu.VMEM((chunks, CHUNK, half), BF16),
            dma((3, experts, 2)),
            dma((3, experts, 2)),
            dma((3, experts, 2)),
            dma((3, experts, 2)),
            dma((2, chunks)),
            dma((2, chunks)),
            dma((2, chunks)),
        ],
        compiler_params=pltpu.CompilerParams(collective_id=0, has_side_effects=True, vmem_limit_bytes=58 * 2**20),
        name="dispatch",
    )(spread, tokens, cotangent)


def normal_parts(value):
    mean = jnp.mean(value, axis=-1, keepdims=True)
    centered = value - mean
    scale = lax.rsqrt(jnp.mean(centered * centered, axis=-1, keepdims=True) + EPS)
    return centered * scale, scale


def norm_back(unit, scale, grad_norm, gain):
    weighted = grad_norm * gain
    return scale * (
        weighted
        - jnp.mean(weighted, axis=-1, keepdims=True)
        - unit * jnp.mean(weighted * unit, axis=-1, keepdims=True)
    )


def hidden_total(term):
    return lax.psum_scatter(term.astype(BF16), "hidden", scatter_dimension=0, tiled=True).astype(F32)


def hidden_all(term):
    return lax.all_gather(term.astype(BF16), "hidden", axis=0, tiled=True)


def gate_piece(rows, state, center):
    share = jax.nn.sigmoid(jnp.sum(rows * center, axis=-1, keepdims=True))
    return share * state + (1.0 - share) * rows


def on_device(experts, places, tokens, dispatch_rows, w_in, w_out, b_in, b_out, ln_gain, ln_bias, centroid, cotangent):
    slots = dispatch_rows[0]
    tok_count, width = tokens.shape
    cap = slots.shape[1]
    x_all, g_all, pos = dispatch(slots, tokens, cotangent, experts, places)
    capp = pos.shape[1]
    rows = x_all.shape[0]
    place = lax.axis_index("hidden")
    own_count = rows // places
    gains, shifts, center, bias_out = ln_gain[0], ln_bias[0], centroid[0], b_out[0]

    def own_part(full):
        return lax.dynamic_slice_in_dim(full, place * own_count, own_count, 0)

    x_full = x_all.astype(F32)
    g_full = g_all.astype(F32)
    x_own, g_own = own_part(x_full), own_part(g_full)
    state_own, state_full = x_own, x_full
    kept = []
    for layer in range(SUBLAYERS):
        unit, scale = normal_parts(state_full)
        normed = (unit * gains[layer] + shifts[layer]).astype(BF16)
        before = dot(normed, w_in[0, layer]) + b_in[0, layer]
        active = jax.nn.gelu(before).astype(BF16)
        state_own = state_own + hidden_total(dot(active, w_out[0, layer])) + bias_out[layer]
        if layer + 1 < SUBLAYERS:
            state_full = hidden_all(state_own).astype(F32)
        kept.append((normed, before, active, own_part(unit), own_part(scale)))
    mixed_own, gate_back = jax.vjp(gate_piece, x_own, state_own, center)
    grad_x_gate, grad_state, grad_center = gate_back(g_own)

    ranks = pos[:, :cap, 0].reshape(experts, places, cap)
    me = lax.axis_index("expert")

    def to_tokens(own):
        full = lax.all_gather(own.astype(BF16), "hidden", axis=0, tiled=True)
        mine = lax.dynamic_index_in_dim(ranks, place, 1, keepdims=False)
        by_source = mine[lax.rem(jnp.arange(experts) - me + experts, experts)]
        sent = full[jnp.maximum(by_source, 0)]
        back = lax.all_to_all(sent, "expert", split_axis=0, concat_axis=0, tiled=True)
        out = jnp.zeros((tok_count + 1, width), BF16)
        return out.at[slots.reshape(-1)].set(back.reshape(-1, width))[:tok_count]

    mixed = to_tokens(mixed_own)
    grad_w_in = [None] * SUBLAYERS
    grad_w_out = [None] * SUBLAYERS
    grad_b_in = [None] * SUBLAYERS
    grad_b_out = [None] * SUBLAYERS
    grad_gain = [None] * SUBLAYERS
    grad_shift = [None] * SUBLAYERS
    for layer in reversed(range(SUBLAYERS)):
        normed, before, active, unit_own, scale_own = kept[layer]
        grad_b_out[layer] = jnp.sum(grad_state, axis=0)
        grad_p = hidden_all(grad_state)
        grad_w_out[layer] = dot_tn(active, grad_p)
        grad_active = dot_nt(grad_p, w_out[0, layer])
        unused, gelu_back = jax.vjp(jax.nn.gelu, before)
        grad_before = gelu_back(grad_active)[0].astype(BF16)
        grad_b_in[layer] = jnp.sum(grad_before.astype(F32), axis=0)
        grad_w_in[layer] = dot_tn(normed, grad_before)
        grad_norm = hidden_total(dot_nt(grad_before, w_in[0, layer]))
        grad_gain[layer] = jnp.sum(grad_norm * unit_own, axis=0)
        grad_shift[layer] = jnp.sum(grad_norm, axis=0)
        grad_state = grad_state + norm_back(unit_own, scale_own, grad_norm, gains[layer])
    grad_tokens = to_tokens(grad_state + grad_x_gate).astype(F32)
    sum_gain, sum_shift, sum_bias, sum_center = lax.psum(
        (jnp.stack(grad_gain), jnp.stack(grad_shift), jnp.stack(grad_b_out), grad_center), "hidden"
    )
    return (
        mixed,
        grad_tokens,
        jnp.stack(grad_w_in)[None],
        jnp.stack(grad_w_out)[None],
        jnp.stack(grad_b_in)[None],
        sum_bias[None],
        sum_gain[None],
        sum_shift[None],
        sum_center[None],
    )


def solution(mesh):
    rows = P(("expert", "hidden"), None)
    return jax.shard_map(
        functools.partial(on_device, mesh.shape["expert"], mesh.shape["hidden"]),
        mesh=mesh,
        in_specs=(
            rows,
            P(("expert", "hidden"), None, None),
            P("expert", None, None, "hidden"),
            P("expert", None, "hidden", None),
            P("expert", None, "hidden"),
            P("expert", None, None),
            P("expert", None, None),
            P("expert", None, None),
            P("expert", None),
            rows,
        ),
        out_specs=(
            rows,
            rows,
            P("expert", None, None, "hidden"),
            P("expert", None, "hidden", None),
            P("expert", None, "hidden"),
            P("expert", None, None),
            P("expert", None, None),
            P("expert", None, None),
            P("expert", None),
        ),
        check_vma=False,
    )
```

```python
import functools

import jax
import jax.numpy as jnp
from jax import lax
from jax.experimental import pallas as pl
from jax.experimental.pallas import tpu as pltpu
from jax.sharding import PartitionSpec as P

MESH = pl.DeviceIdType.MESH
SUBLAYERS = 2
EPS = 1e-05
F32 = jnp.float32
BF16 = jnp.bfloat16
CHUNK = 256
GROUPS = 4
C1 = 0.7978845608028654
C2 = 0.044715


def dot(left, right):
    return jnp.dot(left, right, preferred_element_type=F32)


def dot_tn(left, right):
    return lax.dot_general(left, right, (((0,), (0,)), ((), ())), preferred_element_type=F32)


def dot_nt(left, right):
    return lax.dot_general(left, right, (((1,), (1,)), ((), ())), preferred_element_type=F32)


def row_window(chunk, blocks, cap, rows):
    low = (chunk * CHUNK) // cap
    high = min(blocks - 1, (chunk * CHUNK + CHUNK - 1 + cap * blocks - rows) // cap)
    return low, high + 1


def dispatch_kernel(
    experts, cap, slots, tok, cot, xc, gc, pos, xsend, gsend, csend, xs, gs, cs, xh, gh, ps, pr, fs, fr, hs, hr, ls
):
    me = lax.axis_index("expert")
    place = lax.axis_index("hidden")
    y = place // 2
    c = lax.rem(place, 2)
    over_y = lax.rem(place + 2, 4)
    over_c = place + 1 - 2 * c
    blocks, capp, half = xs.shape
    toks, width = tok.shape
    rows = xc.shape[0]
    chunks = rows // CHUNK

    barrier = pltpu.get_barrier_semaphore()

    def greet(i, carry):
        e = lax.rem(me + i // 2, experts)
        cc = lax.rem(i, 2)

        @pl.when(jnp.logical_or(i // 2 > 0, cc != c))
        def _():
            pl.semaphore_signal(barrier, 1, device_id=(e, 2 * y + cc), device_id_type=MESH)

        return carry

    lax.fori_loop(0, 2 * experts, greet, 0)
    pl.semaphore_signal(barrier, 1, device_id=(me, over_y), device_id_type=MESH)
    pl.semaphore_wait(barrier, 2 * experts)

    sends = (xsend, gsend, csend)
    lands = (xs, gs, cs)

    def rank(d, yy, cc):
        return d * 4 + yy * 2 + cc

    def plane(a, d, cc):
        target = lax.rem(me + experts - d, experts)
        src = csend.at[target] if a == 2 else sends[a].at[cc, target]
        return pltpu.make_async_remote_copy(
            src_ref=src,
            dst_ref=lands[a].at[rank(d, y, c)],
            send_sem=ps.at[a, d, cc],
            recv_sem=pr.at[a, d, c],
            device_id=(target, 2 * y + cc),
            device_id_type=MESH,
        )

    def landed(a, d, cc):
        ref = lands[a].at[rank(d, y, cc)]
        return pltpu.make_async_remote_copy(
            src_ref=ref,
            dst_ref=ref,
            send_sem=ps.at[a, d, cc],
            recv_sem=pr.at[a, d, cc],
            device_id=(me, over_y),
            device_id_type=MESH,
        )

    def forward(a, d, cc):
        ref = lands[a].at[rank(d, y, cc)]
        return pltpu.make_async_remote_copy(
            src_ref=ref,
            dst_ref=ref,
            send_sem=fs.at[a, d, cc],
            recv_sem=fr.at[a, d, cc],
            device_id=(me, over_y),
            device_id_type=MESH,
        )

    def forwarded(a, d, cc):
        ref = lands[a].at[rank(d, 1 - y, cc)]
        return pltpu.make_async_remote_copy(
            src_ref=ref,
            dst_ref=ref,
            send_sem=fs.at[a, d, cc],
            recv_sem=fr.at[a, d, cc],
            device_id=(me, over_y),
            device_id_type=MESH,
        )

    lane = lax.broadcasted_iota(jnp.int32, (capp, 128), 1)
    slot = lax.broadcasted_iota(jnp.int32, (capp, 128), 0)

    def pick(target, source):
        where = slots[target]
        hot = jnp.concatenate([jnp.where(where == lane + 128 * t, 1.0, 0.0).astype(BF16) for t in range(toks // 128)], axis=1)
        return dot(hot, source[...]).astype(BF16)

    def start_x(d, cc):
        plane(2, d, cc).start()
        plane(0, d, cc).start()

    def fill(a, target):
        block = pick(target, cot if a else tok)
        sends[a][0, target] = block[:, :half]
        sends[a][1, target] = block[:, half:]

    def fill_x(target):
        fill(0, target)
        load = jnp.sum(jnp.where(slots[target] < toks, 1.0, 0.0), axis=0, keepdims=True)
        csend[target] = jnp.broadcast_to(load, (16, 128)).astype(BF16)

    fill_x(me)
    start_x(0, 1 - c)
    xs[rank(0, y, c)] = xsend[c, me]
    cs[rank(0, y, c)] = csend[me]
    forward(2, 0, c).start()
    forward(0, 0, c).start()

    def send_x(d, carry):
        fill_x(lax.rem(me + experts - d, experts))
        start_x(d, 0)
        start_x(d, 1)
        return carry

    lax.fori_loop(1, experts, send_x, 0)

    fill(1, me)
    plane(1, 0, 1 - c).start()
    gs[rank(0, y, c)] = gsend[c, me]

    def send_g(d, carry):
        fill(1, lax.rem(me + experts - d, experts))
        plane(1, d, 0).start()
        plane(1, d, 1).start()
        return carry

    lax.fori_loop(1, experts, send_g, 0)

    def pass_on(a, d, cc):
        landed(a, d, cc).wait_recv()
        forward(a, d, cc).start()

    pass_on(2, 0, 1 - c)
    pass_on(0, 0, 1 - c)

    def pass_x(d, carry):
        for cc in range(2):
            pass_on(2, d, cc)
            pass_on(0, d, cc)
        return carry

    lax.fori_loop(1, experts, pass_x, 0)
    forward(1, 0, c).start()
    pass_on(1, 0, 1 - c)

    def pass_g(d, carry):
        for cc in range(2):
            pass_on(1, d, cc)
        return carry

    def await_counts(d, carry):
        for cc in range(2):
            forwarded(2, d, cc).wait_recv()
        return carry

    lax.fori_loop(0, experts, await_counts, 0)

    def place_block(r, start):
        load = cs[r][0:8, :].astype(F32)[0:1, :].astype(jnp.int32)
        pos[r] = jnp.where(slot < load, start + slot, -1)
        return start + load

    lax.fori_loop(0, blocks, place_block, jnp.zeros((1, 128), jnp.int32))

    def pack_out(a, k):
        held = gh if a else xh
        out = gc if a else xc
        spot = out.at[pl.ds(k * CHUNK, CHUNK), pl.ds(pl.multiple_of(c * half, 128), half)]
        return (
            pltpu.make_async_copy(held.at[k], spot, ls.at[a, k]),
            pltpu.make_async_remote_copy(
                src_ref=held.at[k],
                dst_ref=spot,
                send_sem=hs.at[a, k],
                recv_sem=hr.at[a, k],
                device_id=(me, over_c),
                device_id_type=MESH,
            ),
        )

    def pack_in(a, k):
        out = gc if a else xc
        spot = out.at[pl.ds(k * CHUNK, CHUNK), pl.ds(pl.multiple_of((1 - c) * half, 128), half)]
        return pltpu.make_async_remote_copy(
            src_ref=spot,
            dst_ref=spot,
            send_sem=hs.at[a, k],
            recv_sem=hr.at[a, k],
            device_id=(me, over_c),
            device_id_type=MESH,
        )

    def pack(a, k):
        low, high = row_window(k, blocks, cap, rows)
        count = (high - low) * capp
        where = pos[low:high].reshape(count, 128)
        number = lax.broadcasted_iota(jnp.int32, (count, 128), 1) + k * CHUNK
        hot = jnp.concatenate([jnp.where(where == number + 128 * t, 1.0, 0.0).astype(BF16) for t in range(CHUNK // 128)], axis=1)
        held = gh if a else xh
        held[k] = dot_tn(hot, lands[a][low:high].reshape(count, half)).astype(BF16)
        for copy in pack_out(a, k):
            copy.start()

    def await_forwarded(a, low, high):
        def body(d, carry):
            for cc in range(2):
                forwarded(a, d, cc).wait_recv()
            return carry

        lax.fori_loop(low, high, body, 0)

    for a in range(2):
        done = 0
        for k in range(chunks):
            if a == 0:
                lax.fori_loop(1 + (k * (experts - 1)) // chunks, 1 + ((k + 1) * (experts - 1)) // chunks, pass_g, 0)
            need = -(-row_window(k, blocks, cap, rows)[1] // 4)
            await_forwarded(a, done, need)
            done = need
            pack(a, k)

    for a in range(2):
        for k in range(chunks):
            keep, give = pack_out(a, k)
            keep.wait()
            give.wait_send()
            pack_in(a, k).wait_recv()

    def drain(d, carry):
        for a in range(3):
            for cc in range(2):
                forward(a, d, cc).wait_send()
        return carry

    lax.fori_loop(0, experts, drain, 0)
    for a in range(3):
        plane(a, 0, 1 - c).wait_send()

    def drain_plane(d, carry):
        for a in range(3):
            for cc in range(2):
                plane(a, d, cc).wait_send()
        return carry

    lax.fori_loop(1, experts, drain_plane, 0)


def dispatch(spread, cap, tokens, cotangent, places):
    experts, capp = spread.shape[:2]
    toks, width = tokens.shape
    rows = toks * places
    blocks = experts * places
    half = width // 2
    chunks = rows // CHUNK
    vmem = pl.BlockSpec(memory_space=pltpu.VMEM)
    hbm = pl.BlockSpec(memory_space=pl.ANY)
    dma = pltpu.SemaphoreType.DMA
    return pl.pallas_call(
        functools.partial(dispatch_kernel, experts, cap),
        out_shape=(
            jax.ShapeDtypeStruct((rows, width), BF16),
            jax.ShapeDtypeStruct((rows, width), BF16),
            jax.ShapeDtypeStruct((blocks, capp, 128), jnp.int32),
        ),
        in_specs=[vmem, vmem, vmem],
        out_specs=(hbm, hbm, vmem),
        scratch_shapes=[
            pltpu.VMEM((2, experts, capp, half), BF16),
            pltpu.VMEM((2, experts, capp, half), BF16),
            pltpu.VMEM((experts, 16, 128), BF16),
            pltpu.VMEM((blocks, capp, half), BF16),
            pltpu.VMEM((blocks, capp, half), BF16),
            pltpu.VMEM((blocks, 16, 128), BF16),
            pltpu.VMEM((chunks, CHUNK, half), BF16),
            pltpu.VMEM((chunks, CHUNK, half), BF16),
            dma((3, experts, 2)),
            dma((3, experts, 2)),
            dma((3, experts, 2)),
            dma((3, experts, 2)),
            dma((2, chunks)),
            dma((2, chunks)),
            dma((2, chunks)),
        ],
        compiler_params=pltpu.CompilerParams(collective_id=0, has_side_effects=True, vmem_limit_bytes=58 * 2**20),
        name="dispatch",
    )(spread, tokens, cotangent)


def layers_kernel(
    experts,
    cap,
    xc, gc, pos, slots, w_in, w_out, b_in, b_out, gains, shifts, center,
    mixed, gtok, gw_in, gw_out, gb_in, sums, spill, mland,
    win, wout, acc_in, acc_out, xbuf, gbuf, ubuf, nbuf, nscr, ascr, pscr, own, csend, crecv,
    ysend, yrecv, unit1, base, stat, mown, msend, mrecv, packed, posbuf, esend, eown, erecv, mhalf, zland, tally, btally, mine, tallies,
    chunk_sem, group_sem, plane_sem, sum_sem, w_sem, x_sem, g_sem, u_sem, local_sem,
):
    me = lax.axis_index("expert")
    place = lax.axis_index("hidden")
    y = place // 2
    c = lax.rem(place, 2)
    over_y = lax.rem(place + 2, 4)
    over_c = place + 1 - 2 * c
    over_both = 3 - place
    rows, width = xc.shape
    chunks = rows // CHUNK
    hidden = b_in.shape[1]
    half = width // 2
    side = CHUNK // 2
    toks = mixed.shape[0]
    capp = slots.shape[1]
    blocks = 4 * experts
    srecv = (mland, zland)
    groups = GROUPS
    span = experts // groups

    barrier = pltpu.get_barrier_semaphore()

    def greet(i, carry):
        e = lax.rem(me + i // 2, experts)
        cc = lax.rem(i, 2)

        @pl.when(jnp.logical_or(i // 2 > 0, cc != c))
        def _():
            pl.semaphore_signal(barrier, 1, device_id=(e, 2 * y + cc), device_id_type=MESH)

        return carry

    lax.fori_loop(0, 2 * experts, greet, 0)
    pl.semaphore_signal(barrier, 1, device_id=(me, over_y), device_id_type=MESH)
    pl.semaphore_signal(barrier, 1, device_id=(me, over_both), device_id_type=MESH)

    own_rows = pl.ds(pl.multiple_of(c * side, side), side)
    other_rows = pl.ds(pl.multiple_of((1 - c) * side, side), side)
    own_cols = pl.ds(pl.multiple_of(c * half, half), half)
    other_cols = pl.ds(pl.multiple_of((1 - c) * half, half), half)

    def send(src, dst, kind, k, to):
        return pltpu.make_async_remote_copy(
            src_ref=src,
            dst_ref=dst,
            send_sem=chunk_sem.at[kind, 0, k],
            recv_sem=chunk_sem.at[kind, 1, k],
            device_id=(me, to),
            device_id_type=MESH,
        )

    P_CORE, P_Y, N_CORE, M_CORE, D_CORE, D_Y, DP_CORE, Z_CORE = range(8)

    def p_core(k):
        return send(csend.at[lax.rem(k, 2)], crecv.at[k], P_CORE, k, over_c)

    def d_core(k):
        return send(csend.at[lax.rem(k, 2)], crecv.at[k], D_CORE, k, over_c)

    def p_y(k):
        return send(ysend.at[0, k], yrecv.at[0, k], P_Y, k, over_y)

    def d_y(k):
        return send(ysend.at[1, k], yrecv.at[1, k], D_Y, k, over_y)

    def n_core(k, part):
        return send(nbuf.at[k, part], nbuf.at[k, part], N_CORE, k, over_c)

    def dp_core(k, part):
        return send(nbuf.at[k, part], nbuf.at[k, part], DP_CORE, k, over_c)

    def m_core(k):
        return send(msend.at[lax.rem(k, 2)], mrecv.at[k], M_CORE, k, over_c)

    def z_core(k):
        return send(msend.at[lax.rem(k, 2)], mrecv.at[k], Z_CORE, k, over_c)

    def load_x(k):
        return pltpu.make_async_copy(xc.at[pl.ds(k * CHUNK, CHUNK)], xbuf.at[lax.rem(k, 3)], x_sem.at[lax.rem(k, 3)])

    def load_g(k):
        return pltpu.make_async_copy(gc.at[pl.ds(k * CHUNK, CHUNK)], gbuf.at[lax.rem(k, 3)], g_sem.at[lax.rem(k, 3)])

    def save_u(k):
        return pltpu.make_async_copy(ubuf.at[lax.rem(k, 2)], spill.at[k], u_sem.at[lax.rem(k, 2)])

    def load_u(k):
        return pltpu.make_async_copy(spill.at[k], ubuf.at[lax.rem(k, 2)], u_sem.at[lax.rem(k, 2)])

    def load_w(layer):
        return (
            pltpu.make_async_copy(w_in.at[layer], win.at[layer], w_sem.at[layer, 0]),
            pltpu.make_async_copy(w_out.at[layer], wout.at[layer], w_sem.at[layer, 1]),
        )

    for layer in range(SUBLAYERS):
        for copy in load_w(layer):
            copy.start()
    load_x(0).start()
    tally[...] = jnp.zeros_like(tally)
    btally[...] = jnp.zeros_like(btally)

    def clear(acc):
        def body(i, carry):
            acc[pl.ds(pl.multiple_of(i * 32, 32), 32)] = jnp.zeros((32, acc.shape[1]), F32)
            return carry

        lax.fori_loop(0, acc.shape[0] // 32, body, 0)

    clear(acc_in)
    clear(acc_out)
    pl.semaphore_wait(barrier, 2 * experts + 1)

    STEP = 32

    def over_rows(count, body):
        def step(i, carry):
            body(pl.multiple_of(i * STEP, STEP))
            return carry

        lax.fori_loop(0, count // STEP, step, 0)

    def row_stats(v):
        mean = jnp.mean(v, axis=-1, keepdims=True)
        v = v - mean
        scale = lax.rsqrt(jnp.mean(v * v, axis=-1, keepdims=True) + EPS)
        return v * scale, scale

    def tiles(n):
        return [slice(t * 256, (t + 1) * 256) for t in range(n // 256)]

    def first(layer, normed, slot):
        for f in tiles(hidden):
            a = dot(normed(), win[layer, :, f]) + b_in[layer : layer + 1, f]
            sq = a * a
            t = jnp.tanh(a * (C1 + (C1 * C2) * sq))
            up = 0.5 + 0.5 * t
            ubuf[slot, 0, :, f] = (a * up).astype(BF16)
            ubuf[slot, 1, :, f] = (up + (0.5 * a) * (1.0 - t * t) * (C1 + (3.0 * C1 * C2) * sq)).astype(BF16)

    def second(layer, slot):
        for d in tiles(width):
            pscr[:, d] = dot(ubuf[slot, 0], wout[layer, :, d])

    def back(layer, grad, slot):
        for f in tiles(hidden):
            da = (dot_nt(grad(), wout[layer, f, :]) * ubuf[slot, 1, :, f].astype(F32)).astype(BF16)
            ascr[:, f] = da
            btally[layer, :, f] += fold(da.astype(F32))
        for d in tiles(width):
            pscr[:, d] = dot_nt(ascr[...], win[layer, d, :])

    def weight_grads(normed, grad, slot):
        for f in tiles(hidden):
            acc_out[f, :] += dot_tn(ubuf[slot, 0, :, f], grad())
        for d in tiles(width):
            acc_in[d, :] += dot_tn(normed(d), ascr[...])

    def split_rows(k, ring):
        own[ring] = pscr[own_rows]
        csend[ring] = pscr[other_rows].astype(BF16)

    def split_cols(ring):
        mown[...] = pscr[:, own_cols]
        msend[ring] = pscr[:, other_cols].astype(BF16)

    def fold(value):
        return jnp.sum(value.reshape(value.shape[0] // 8, 8, value.shape[1]), axis=0)

    def add_row(row, value):
        tally[row] += fold(value)

    GAIN0, GAIN1, SHIFT0, SHIFT1, BOUT0, BOUT1, CENT = range(7)

    def stage_a(k):
        ring, slot = lax.rem(k, 2), lax.rem(k, 3)

        def body(r):
            v = xbuf[slot, pl.ds(r, STEP)].astype(F32)
            share = jax.nn.sigmoid(jnp.sum(v * center[...], axis=-1, keepdims=True))
            stat[k, pl.ds(r, STEP), 0:1] = share
            unit, _ = row_stats(v)
            nscr[pl.ds(r, STEP)] = (unit * gains[0:1] + shifts[0:1]).astype(BF16)

        over_rows(CHUNK, body)

        @pl.when(k >= 2)
        def _():
            save_u(k - 2).wait()
            p_core(k - 2).wait_send()

        first(0, lambda: nscr[...], ring)
        save_u(k).start()
        second(0, ring)
        split_rows(k, ring)
        p_core(k).start()

    def stage_sum(k, core, over, which):
        core(k).wait_recv()
        ysend[which, k] = (own[lax.rem(k, 2)] + crecv[k].astype(F32)).astype(BF16)
        over(k).start()

    def loop1(k, carry):
        @pl.when(k < chunks)
        def _():
            load_x(k).wait()

        @pl.when(k + 1 < chunks)
        def _():
            load_x(k + 1).start()

        @pl.when(k < chunks)
        def _():
            stage_a(k)

        @pl.when(k >= 1)
        def _():
            stage_sum(k - 1, p_core, p_y, 0)

        return carry

    for copy in load_w(0):
        copy.wait()
    lax.fori_loop(0, chunks + 1, loop1, 0)
    for k in (chunks - 2, chunks - 1):
        save_u(k).wait()
        p_core(k).wait_send()
    load_x(0).start()
    load_g(0).start()
    for copy in load_w(1):
        copy.wait()

    def stage_c(k):
        ring, slot = lax.rem(k, 2), lax.rem(k, 3)
        p_y(k).wait_recv()

        def body(r):
            here = pl.ds(r, STEP)
            there = pl.ds(pl.multiple_of(c * side + r, STEP), STEP)
            x = xbuf[slot, there].astype(F32)
            g = gbuf[slot, there].astype(F32)
            share = stat[k, there, 0:1]
            state = x + (ysend[0, k, here].astype(F32) + yrecv[0, k, here].astype(F32)) + b_out[0:1]
            unit, scale = row_stats(state)
            unit1[k, here] = unit.astype(BF16)
            stat[k, there, 2:3] = scale
            nbuf[k, c, here] = (unit * gains[1:2] + shifts[1:2]).astype(BF16)
            diff = state + b_out[1:2] - x
            base[ring, here] = 0.5 * (share * diff + x)
            pull = jnp.sum(g * diff, axis=-1, keepdims=True)
            stat[k, there, 1:2] = 0.5 * share * (1.0 - share) * pull

        over_rows(side, body)
        n_core(k, c).start()
        stat[k, other_rows, 1:2] = jnp.zeros((side, 1), F32)

    def stage_d(k):
        ring, slot = lax.rem(k, 2), lax.rem(k, 3)
        n_core(k, 1 - c).wait_recv()
        normed = lambda: nbuf[k].reshape(CHUNK, width)
        first(1, normed, 0)
        second(1, 0)

        def body(r, based):
            at = (c if based else 1 - c) * side + r
            there = pl.ds(pl.multiple_of(at, STEP), STEP)
            g = gbuf[slot, there].astype(F32)
            share = stat[k, there, 0:1]
            p = pscr[there]
            pull = jnp.sum(g * p, axis=-1, keepdims=True)
            stat[k, there, 1:2] = stat[k, there, 1:2] + share * (1.0 - share) * pull
            out = share * p
            if based:
                out = out + base[ring, pl.ds(r, STEP)]
            pscr[there] = out
            grad = share * g
            nscr[there] = grad.astype(BF16)
            add_row(BOUT1, 0.25 * grad)

        over_rows(side, functools.partial(body, based=True))
        over_rows(side, functools.partial(body, based=False))

        @pl.when(k >= 2)
        def _():
            m_core(k - 2).wait_send()
            d_core(k - 2).wait_send()

        split_cols(ring)
        m_core(k).start()
        back(1, lambda: nscr[...], 0)
        split_rows(k, ring)
        d_core(k).start()
        weight_grads(lambda d: nbuf[k, :, :, d].reshape(CHUNK, 256), lambda: nscr[...], 0)

    def stage_pack(k, core):
        core(k).wait_recv()
        packed[k] = (mown[...] + mrecv[k].astype(F32)).astype(BF16)

    def group_copy(a, g):
        part = pl.ds(g * span, span)
        return pltpu.make_async_remote_copy(
            src_ref=esend.at[part],
            dst_ref=erecv.at[a, part],
            send_sem=group_sem.at[a, 0, g],
            recv_sem=group_sem.at[a, 1, g],
            device_id=(me, over_y),
            device_id_type=MESH,
        )

    def plane_copy(a, d, cc):
        target = lax.rem(me + d, experts)
        return pltpu.make_async_remote_copy(
            src_ref=eown.at[d, cc],
            dst_ref=srecv[a].at[c, me],
            send_sem=plane_sem.at[a, 0, d, cc],
            recv_sem=plane_sem.at[a, 1, d, c],
            device_id=(target, 2 * y + cc),
            device_id_type=MESH,
        )

    def plane_landed(a, d, cc):
        source = lax.rem(me + experts - d, experts)
        ref = srecv[a].at[cc, source]
        return pltpu.make_async_remote_copy(
            src_ref=ref,
            dst_ref=ref,
            send_sem=plane_sem.at[a, 0, d, cc],
            recv_sem=plane_sem.at[a, 1, d, cc],
            device_id=(me, over_y),
            device_id_type=MESH,
        )

    def group_rows(g):
        low = max(0, rows - cap * blocks + cap * 4 * g * span) // CHUNK
        high = min(chunks, -(-(cap * 4 * (g + 1) * span) // CHUNK))
        return low, high

    def expand(g, a):
        low, high = group_rows(g)
        copy = pltpu.make_async_copy(pos.at[pl.ds(4 * g * span, 4 * span)], posbuf, local_sem.at[0])
        copy.start()
        copy.wait()
        if a:
            group_copy(0, g).wait_send()
        number = lax.broadcasted_iota(jnp.int32, (2 * capp, 128), 1) + low * CHUNK

        def part(i, yy, into):
            where = posbuf[pl.ds(4 * i + 2 * yy, 2)].reshape(2 * capp, 128)
            hot = jnp.concatenate(
                [jnp.where(where == number + 128 * t, 1.0, 0.0).astype(BF16) for t in range((high - low) * CHUNK // 128)], axis=1
            )
            block = dot(hot, packed[low:high].reshape((high - low) * CHUNK, half))
            into[g * span + i] = block.astype(BF16).reshape(2, capp, half)

        def far(i, carry):
            part(i, 1 - y, esend)
            return carry

        def near(i, carry):
            if a:
                finish(0, g * span + i)
            part(i, y, eown)
            return carry

        lax.fori_loop(0, span, far, 0)
        group_copy(a, g).start()
        lax.fori_loop(0, span, near, 0)

    def self_copy(a):
        return pltpu.make_async_copy(eown.at[0, c], srecv[a].at[c, me], local_sem.at[1])

    def finish(a, d):
        @pl.when(d > 0)
        def _():
            plane_copy(a, d, 0).wait_send()
            plane_copy(a, d, 1).wait_send()

        @pl.when(d == 0)
        def _():
            plane_copy(a, 0, 1 - c).wait_send()
            self_copy(a).wait()

    def give_back(a, g):
        group_copy(a, g).wait_recv()

        def one(i, carry):
            d = g * span + i
            eown[d] = (eown[d].astype(F32) + erecv[a, d].astype(F32)).astype(BF16)

            @pl.when(d > 0)
            def _():
                plane_copy(a, d, 0).start()
                plane_copy(a, d, 1).start()

            @pl.when(d == 0)
            def _():
                plane_copy(a, 0, 1 - c).start()
                self_copy(a).start()

            return carry

        lax.fori_loop(0, span, one, 0)

    ready = [group_rows(g)[1] for g in range(groups)]

    def loop2(k, carry):
        @pl.when(k < chunks)
        def _():
            load_x(k).wait()
            load_g(k).wait()

        @pl.when(k + 1 < chunks)
        def _():
            load_x(k + 1).start()
            load_g(k + 1).start()

        @pl.when(k >= 2)
        def _():
            stage_sum(k - 2, d_core, d_y, 1)

        @pl.when(k < chunks)
        def _():
            stage_c(k)

        @pl.when(k >= 2)
        def _():
            stage_pack(k - 2, m_core)

        for g in range(groups):
            if ready[g] < chunks:

                @pl.when(k - 1 == ready[g])
                def _():
                    expand(g, 0)

        @pl.when(jnp.logical_and(k >= 1, k <= chunks))
        def _():
            stage_d(k - 1)

        return carry

    lax.fori_loop(0, chunks + 2, loop2, 0)
    for k in (chunks - 2, chunks - 1):
        m_core(k).wait_send()
        d_core(k).wait_send()

    def save_grads(layer):
        return (
            pltpu.make_async_copy(acc_in, gw_in.at[layer], w_sem.at[layer, 0]),
            pltpu.make_async_copy(acc_out, gw_out.at[layer], w_sem.at[layer, 1]),
        )

    for copy in save_grads(1):
        copy.start()
    load_x(0).start()
    load_g(0).start()
    load_u(0).start()
    for g in range(groups):
        if ready[g] >= chunks:
            expand(g, 0)
    for copy in save_grads(1):
        copy.wait()
    clear(acc_in)
    clear(acc_out)

    def stage_g(k):
        ring, slot = lax.rem(k, 2), lax.rem(k, 3)
        d_y(k).wait_recv()
        n_core(k, c).wait_send()

        def body(r):
            here = pl.ds(r, STEP)
            there = pl.ds(pl.multiple_of(c * side + r, STEP), STEP)
            g = gbuf[slot, there].astype(F32)
            share = stat[k, there, 0:1]
            dn = ysend[1, k, here].astype(F32) + yrecv[1, k, here].astype(F32)
            unit = unit1[k, here].astype(F32)
            w = dn * gains[1:2]
            add_row(GAIN1, 0.5 * dn * unit)
            add_row(SHIFT1, 0.5 * dn)
            grad = share * g + stat[k, there, 2:3] * (
                w - jnp.mean(w, axis=-1, keepdims=True) - unit * jnp.mean(w * unit, axis=-1, keepdims=True)
            )
            nbuf[k, c, here] = grad.astype(BF16)
            add_row(BOUT0, 0.5 * grad)
            base[ring, here] = 0.5 * (grad + (1.0 - share) * g)

        over_rows(side, body)
        dp_core(k, c).start()

    def stage_h(k):
        ring, slot = lax.rem(k, 2), lax.rem(k, 3)
        dp_core(k, 1 - c).wait_recv()
        back(0, lambda: nbuf[k].reshape(CHUNK, width), ring)

        def body(r, based):
            at = (c if based else 1 - c) * side + r
            there = pl.ds(pl.multiple_of(at, STEP), STEP)
            x = xbuf[slot, there].astype(F32)
            pull = stat[k, there, 1:2]
            unit, scale = row_stats(x)
            nscr[there] = (unit * gains[0:1] + shifts[0:1]).astype(BF16)
            dn = pscr[there]
            w = dn * gains[0:1]
            add_row(GAIN0, dn * unit)
            add_row(SHIFT0, dn)
            add_row(CENT, pull * x)
            out = pull * center[...] + scale * (
                w - jnp.mean(w, axis=-1, keepdims=True) - unit * jnp.mean(w * unit, axis=-1, keepdims=True)
            )
            if based:
                out = out + base[ring, pl.ds(r, STEP)]
            pscr[there] = out

        over_rows(side, functools.partial(body, based=True))
        over_rows(side, functools.partial(body, based=False))

        @pl.when(k >= 2)
        def _():
            z_core(k - 2).wait_send()

        split_cols(ring)
        z_core(k).start()

    def stage_w(k):
        weight_grads(lambda d: nscr[:, d], lambda: nbuf[k].reshape(CHUNK, width), lax.rem(k, 2))

    def loop3(k, carry):
        @pl.when(k < chunks)
        def _():
            load_x(k).wait()
            load_g(k).wait()

        @pl.when(k + 1 < chunks)
        def _():
            load_x(k + 1).start()
            load_g(k + 1).start()

        @pl.when(k >= 2)
        def _():
            stage_pack(k - 2, z_core)

        @pl.when(k < chunks)
        def _():
            stage_g(k)

        @pl.when(k >= 1)
        def _():
            load_u(k - 1).wait()

        @pl.when(jnp.logical_and(k >= 1, k < chunks))
        def _():
            load_u(k).start()

        @pl.when(k >= 1)
        def _():
            stage_h(k - 1)

        for g in range(groups):

            @pl.when(k == 1 + g * (chunks // groups))
            def _():
                give_back(0, g)

        for g in range(groups):
            if ready[g] < chunks:

                @pl.when(k - 1 == ready[g])
                def _():
                    expand(g, 1)

        @pl.when(jnp.logical_and(k >= 1, k < chunks))
        def _():
            stage_w(k - 1)

        return carry

    lax.fori_loop(0, chunks + 1, loop3, 0)
    stage_pack(chunks - 1, z_core)
    for g in range(groups):
        if ready[g] >= chunks:
            expand(g, 1)
    stage_w(chunks - 1)
    for copy in save_grads(0):
        copy.start()

    for row in range(8):
        mine[row : row + 1] = jnp.sum(tally[row], axis=0, keepdims=True)
    for layer in range(SUBLAYERS):
        gb_in[layer : layer + 1] = jnp.sum(btally[layer], axis=0, keepdims=True)
    tallies[place] = mine[...]

    def tally_copy(i, to):
        return pltpu.make_async_remote_copy(
            src_ref=mine,
            dst_ref=tallies.at[place],
            send_sem=sum_sem.at[0, i],
            recv_sem=sum_sem.at[1, i],
            device_id=(me, to),
            device_id_type=MESH,
        )

    def tally_landed(i, frm):
        ref = tallies.at[frm]
        return pltpu.make_async_remote_copy(
            src_ref=ref, dst_ref=ref, send_sem=sum_sem.at[0, i], recv_sem=sum_sem.at[1, i], device_id=(me, frm), device_id_type=MESH
        )

    others = (over_c, over_y, over_both)
    for i, to in enumerate(others):
        tally_copy(i, to).start()
    for g in range(groups):
        give_back(1, g)

    def gather_back(a, result):
        def wait(d, carry):
            for cc in range(2):

                @pl.when(jnp.logical_or(d > 0, cc != c))
                def _():
                    plane_landed(a, d, cc).wait_recv()

            return carry

        lax.fori_loop(0, experts, wait, 0)
        if a:
            self_copy(1).wait()
        lane = lax.broadcasted_iota(jnp.int32, (experts * capp, 128), 1)
        where = slots[...].reshape(experts * capp, 128)
        for j in range(2):
            if a == 0:
                copy = pltpu.make_async_copy(mland.at[j], mhalf, local_sem.at[0])
                copy.start()
                copy.wait()
            for i, hold in enumerate((nscr, ascr)):
                hot = jnp.concatenate(
                    [jnp.where(where == lane + (i * CHUNK + 128 * t), 1.0, 0.0).astype(BF16) for t in range(CHUNK // 128)], axis=1
                )
                block = mhalf[...] if a == 0 else zland[j]
                hold[:, j * half : (j + 1) * half] = dot_tn(hot, block.reshape(experts * capp, half)).astype(BF16)
        for i, hold in enumerate((nscr, ascr)):
            pltpu.make_async_copy(hold, result.at[pl.ds(i * CHUNK, CHUNK)], local_sem.at[2 + i]).start()

    def gathered(result):
        for i, hold in enumerate((nscr, ascr)):
            pltpu.make_async_copy(hold, result.at[pl.ds(i * CHUNK, CHUNK)], local_sem.at[2 + i]).wait()

    gather_back(0, mixed)
    for i, frm in enumerate(others):
        tally_landed(i, frm).wait_recv()
        tally_copy(i, frm).wait_send()
    sums[...] = (tallies[0] + tallies[1]) + (tallies[2] + tallies[3])
    gathered(mixed)
    gather_back(1, gtok)
    for g in range(groups):
        group_copy(1, g).wait_send()

    def last(d, carry):
        @pl.when(d > 0)
        def _():
            plane_copy(1, d, 0).wait_send()
            plane_copy(1, d, 1).wait_send()

        @pl.when(d == 0)
        def _():
            plane_copy(1, 0, 1 - c).wait_send()

        return carry

    lax.fori_loop(0, experts, last, 0)

    def last_chunk(k, carry):
        p_y(k).wait_send()
        d_y(k).wait_send()
        dp_core(k, c).wait_send()
        return carry

    lax.fori_loop(0, chunks, last_chunk, 0)
    for k in (chunks - 2, chunks - 1):
        z_core(k).wait_send()
    for copy in save_grads(0):
        copy.wait()
    gathered(gtok)


def layers(cap, xc, gc, pos, slots, w_in, w_out, b_in, b_out, gains, shifts, center, toks):
    experts, capp = slots.shape[:2]
    blocks = pos.shape[0]
    rows, width = xc.shape
    hidden = b_in.shape[1]
    half, side, chunks = width // 2, CHUNK // 2, rows // CHUNK
    span = experts // GROUPS
    vmem = pl.BlockSpec(memory_space=pltpu.VMEM)
    hbm = pl.BlockSpec(memory_space=pl.ANY)
    dma = pltpu.SemaphoreType.DMA
    return pl.pallas_call(
        functools.partial(layers_kernel, experts, cap),
        out_shape=(
            jax.ShapeDtypeStruct((toks, width), BF16),
            jax.ShapeDtypeStruct((toks, width), BF16),
            jax.ShapeDtypeStruct((SUBLAYERS, width, hidden), F32),
            jax.ShapeDtypeStruct((SUBLAYERS, hidden, width), F32),
            jax.ShapeDtypeStruct((SUBLAYERS, hidden), F32),
            jax.ShapeDtypeStruct((8, width), F32),
            jax.ShapeDtypeStruct((chunks, 2, CHUNK, hidden), BF16),
            jax.ShapeDtypeStruct((2, experts, capp, half), BF16),
        ),
        in_specs=[hbm, hbm, hbm, vmem, hbm, hbm, vmem, vmem, vmem, vmem, vmem],
        out_specs=(hbm, hbm, hbm, hbm, vmem, vmem, hbm, hbm),
        scratch_shapes=[
            pltpu.VMEM((SUBLAYERS, width, hidden), BF16),
            pltpu.VMEM((SUBLAYERS, hidden, width), BF16),
            pltpu.VMEM((width, hidden), F32),
            pltpu.VMEM((hidden, width), F32),
            pltpu.VMEM((3, CHUNK, width), BF16),
            pltpu.VMEM((3, CHUNK, width), BF16),
            pltpu.VMEM((2, 2, CHUNK, hidden), BF16),
            pltpu.VMEM((chunks, 2, side, width), BF16),
            pltpu.VMEM((CHUNK, width), BF16),
            pltpu.VMEM((CHUNK, hidden), BF16),
            pltpu.VMEM((CHUNK, width), F32),
            pltpu.VMEM((2, side, width), F32),
            pltpu.VMEM((2, side, width), BF16),
            pltpu.VMEM((chunks, side, width), BF16),
            pltpu.VMEM((2, chunks, side, width), BF16),
            pltpu.VMEM((2, chunks, side, width), BF16),
            pltpu.VMEM((chunks, side, width), BF16),
            pltpu.VMEM((2, side, width), F32),
            pltpu.VMEM((chunks, CHUNK, 128), F32),
            pltpu.VMEM((CHUNK, half), F32),
            pltpu.VMEM((2, CHUNK, half), BF16),
            pltpu.VMEM((chunks, CHUNK, half), BF16),
            pltpu.VMEM((chunks, CHUNK, half), BF16),
            pltpu.VMEM((4 * span, capp, 128), jnp.int32),
            pltpu.VMEM((experts, 2, capp, half), BF16),
            pltpu.VMEM((experts, 2, capp, half), BF16),
            pltpu.VMEM((2, experts, 2, capp, half), BF16),
            pltpu.VMEM((experts, capp, half), BF16),
            pltpu.VMEM((2, experts, capp, half), BF16),
            pltpu.VMEM((8, 8, width), F32),
            pltpu.VMEM((SUBLAYERS, 8, hidden), F32),
            pltpu.VMEM((8, width), F32),
            pltpu.VMEM((4, 8, width), F32),
            dma((8, 2, chunks)),
            dma((2, 2, GROUPS)),
            dma((2, 2, experts, 2)),
            dma((2, 3)),
            dma((SUBLAYERS, 2)),
            dma((3,)),
            dma((3,)),
            dma((2,)),
            dma((4,)),
        ],
        compiler_params=pltpu.CompilerParams(collective_id=1, has_side_effects=True, vmem_limit_bytes=62 * 2**20),
        name="layers",
    )(xc, gc, pos, slots, w_in, w_out, b_in, b_out, gains, shifts, center)


def on_device(experts, places, tokens, dispatch_rows, w_in, w_out, b_in, b_out, ln_gain, ln_bias, centroid, cotangent):
    slots = dispatch_rows[0]
    toks = tokens.shape[0]
    cap = slots.shape[1]
    capp = -(-cap // 16) * 16
    padded = jnp.pad(slots, ((0, 0), (0, capp - cap)), constant_values=toks)
    spread = jnp.broadcast_to(padded[:, :, None], (experts, capp, 128))
    xc, gc, pos = dispatch(spread, cap, tokens, cotangent, places)
    mixed, gtok, gw_in, gw_out, gb_in, sums, _, _ = layers(
        cap, xc, gc, pos, spread, w_in[0], w_out[0], b_in[0], b_out[0], ln_gain[0], ln_bias[0], centroid, toks
    )
    return (
        mixed,
        gtok.astype(F32),
        gw_in[None],
        gw_out[None],
        gb_in[None],
        sums[None, 4:6],
        sums[None, 0:2],
        sums[None, 2:4],
        sums[6:7],
    )


def solution(mesh):
    rows = P(("expert", "hidden"), None)
    return jax.shard_map(
        functools.partial(on_device, mesh.shape["expert"], mesh.shape["hidden"]),
        mesh=mesh,
        in_specs=(
            rows,
            P(("expert", "hidden"), None, None),
            P("expert", None, None, "hidden"),
            P("expert", None, "hidden", None),
            P("expert", None, "hidden"),
            P("expert", None, None),
            P("expert", None, None),
            P("expert", None, None),
            P("expert", None),
            rows,
        ),
        out_specs=(
            rows,
            rows,
            P("expert", None, None, "hidden"),
            P("expert", None, "hidden", None),
            P("expert", None, "hidden"),
            P("expert", None, None),
            P("expert", None, None),
            P("expert", None, None),
            P("expert", None),
        ),
        check_vma=False,
    )
```

```python
import functools

import jax
import jax.numpy as jnp
from jax import lax
from jax.experimental import pallas as pl
from jax.experimental.pallas import tpu as pltpu
from jax.sharding import PartitionSpec as P

MESH = pl.DeviceIdType.MESH
SUBLAYERS = 2
EPS = 1e-05
F32 = jnp.float32
BF16 = jnp.bfloat16
CHUNK = 256
GROUPS = 4
C1 = 0.7978845608028654
C2 = 0.044715


def dot(left, right):
    return jnp.dot(left, right, preferred_element_type=F32)


def dot_tn(left, right):
    return lax.dot_general(left, right, (((0,), (0,)), ((), ())), preferred_element_type=F32)


def dot_nt(left, right):
    return lax.dot_general(left, right, (((1,), (1,)), ((), ())), preferred_element_type=F32)


def row_window(chunk, blocks, cap, rows):
    low = (chunk * CHUNK) // cap
    high = min(blocks - 1, (chunk * CHUNK + CHUNK - 1 + cap * blocks - rows) // cap)
    return low, high + 1


def layers_kernel(
    experts,
    cap,
    slots, tok, cot, w_in, w_out, b_in, b_out, gains, shifts, center,
    mixed, gtok, gw, gb_in, sums, spill, back_rows, land, xc, gc,
    wbuf, acc_in, acc_out, xbuf, gbuf, window, starts, loads, tell, ubuf, nbuf, nscr, ascr, pscr, own, csend, crecv,
    ysend, yrecv, unit1, base, stat, mown, msend, mrecv, packed, esend, eown, erecv, tally, btally, mine, tallies,
    chunk_sem, group_sem, plane_sem, sum_sem, w_sem, x_sem, g_sem, u_sem, local_sem, in_sem, half_sem,
):
    me = lax.axis_index("expert")
    place = lax.axis_index("hidden")
    y = place // 2
    c = lax.rem(place, 2)
    over_y = lax.rem(place + 2, 4)
    over_c = place + 1 - 2 * c
    over_both = 3 - place
    rows, width = xc.shape
    chunks = rows // CHUNK
    hidden = b_in.shape[1]
    half = width // 2
    side = CHUNK // 2
    toks = mixed.shape[0]
    capp = slots.shape[1]
    blocks = 4 * experts
    groups = GROUPS
    span = experts // groups

    barrier = pltpu.get_barrier_semaphore()

    def greet(i, carry):
        e = lax.rem(me + i // 2, experts)
        cc = lax.rem(i, 2)

        @pl.when(jnp.logical_or(i // 2 > 0, cc != c))
        def _():
            pl.semaphore_signal(barrier, 1, device_id=(e, 2 * y + cc), device_id_type=MESH)

        return carry

    lax.fori_loop(0, 2 * experts, greet, 0)
    pl.semaphore_signal(barrier, 1, device_id=(me, over_y), device_id_type=MESH)
    pl.semaphore_signal(barrier, 1, device_id=(me, over_both), device_id_type=MESH)

    own_rows = pl.ds(pl.multiple_of(c * side, side), side)
    other_rows = pl.ds(pl.multiple_of((1 - c) * side, side), side)
    own_cols = pl.ds(pl.multiple_of(c * half, half), half)
    other_cols = pl.ds(pl.multiple_of((1 - c) * half, half), half)

    def send(src, dst, kind, k, to):
        return pltpu.make_async_remote_copy(
            src_ref=src,
            dst_ref=dst,
            send_sem=chunk_sem.at[kind, 0, k],
            recv_sem=chunk_sem.at[kind, 1, k],
            device_id=(me, to),
            device_id_type=MESH,
        )

    P_CORE, P_Y, N_CORE, M_CORE, D_CORE, D_Y, DP_CORE, Z_CORE = range(8)

    def p_core(k):
        return send(csend.at[lax.rem(k, 2)], crecv.at[lax.rem(k, 4)], P_CORE, k, over_c)

    def d_core(k):
        return send(csend.at[lax.rem(k, 2)], crecv.at[lax.rem(k, 4)], D_CORE, k, over_c)

    def p_y(k):
        return send(ysend.at[0, k], yrecv.at[0, k], P_Y, k, over_y)

    def d_y(k):
        return send(ysend.at[1, k], yrecv.at[1, k], D_Y, k, over_y)

    def n_core(k, part):
        return send(nbuf.at[k, part], nbuf.at[k, part], N_CORE, k, over_c)

    def dp_core(k, part):
        return send(nbuf.at[k, part], nbuf.at[k, part], DP_CORE, k, over_c)

    def m_core(k):
        return send(msend.at[lax.rem(k, 2)], mrecv.at[lax.rem(k, 4)], M_CORE, k, over_c)

    def z_core(k):
        return send(msend.at[lax.rem(k, 2)], mrecv.at[lax.rem(k, 4)], Z_CORE, k, over_c)

    def load_x(k):
        return pltpu.make_async_copy(xc.at[pl.ds(k * CHUNK, CHUNK)], xbuf.at[lax.rem(k, 3)], x_sem.at[lax.rem(k, 3)])

    def load_g(k):
        return pltpu.make_async_copy(gc.at[pl.ds(k * CHUNK, CHUNK)], gbuf.at[lax.rem(k, 3)], g_sem.at[lax.rem(k, 3)])

    def save_g(k):
        return pltpu.make_async_copy(gbuf.at[lax.rem(k, 3)], gc.at[pl.ds(k * CHUNK, CHUNK)], g_sem.at[lax.rem(k, 3)])

    def save_x(k):
        return pltpu.make_async_copy(xbuf.at[lax.rem(k, 3)], xc.at[pl.ds(k * CHUNK, CHUNK)], x_sem.at[lax.rem(k, 3)])

    def save_u(k):
        return pltpu.make_async_copy(ubuf.at[lax.rem(k, 2)], spill.at[k], u_sem.at[lax.rem(k, 2), 0])

    def load_u(k):
        return pltpu.make_async_copy(spill.at[k, 0], ubuf.at[lax.rem(k, 2), 0], u_sem.at[lax.rem(k, 2), 0])

    def load_un(k):
        return pltpu.make_async_copy(spill.at[k, pl.ds(1, 2)], ubuf.at[lax.rem(k, 2), pl.ds(1, 2)], u_sem.at[lax.rem(k, 2), 0])

    def load_w(layer):
        return (
            pltpu.make_async_copy(w_in.at[layer], wbuf.at[layer, 0], w_sem.at[layer, 0]),
            pltpu.make_async_copy(w_out.at[layer], wbuf.at[layer, 1], w_sem.at[layer, 1]),
        )

    for layer in range(SUBLAYERS):
        for copy in load_w(layer):
            copy.start()
    pieces = toks // CHUNK
    load_rows = [
        pltpu.make_async_copy(ref.at[pl.ds(i * CHUNK, CHUNK)], ubuf.at[a, i], u_sem.at[a, i])
        for a, ref in enumerate((tok, cot))
        for i in range(pieces)
    ]
    for copy in load_rows:
        copy.start()
    tally[...] = jnp.zeros_like(tally)
    btally[...] = jnp.zeros_like(btally)

    def clear(acc):
        def body(i, carry):
            acc[pl.ds(pl.multiple_of(i * 32, 32), 32)] = jnp.zeros((32, acc.shape[1]), F32)
            return carry

        lax.fori_loop(0, acc.shape[0] // 32, body, 0)

    clear(acc_in)
    clear(acc_out)
    bits = experts.bit_length() - 1

    def partner(i):
        return sum(lax.rem(me // 2**j + i // 2 ** (bits - 1 - j), 2) * 2**j for j in range(bits))


    X, G, COUNT = range(3)
    picked = (esend, eown)

    def rank(i, yy, cc):
        return i * 4 + yy * 2 + cc

    def count_tile(r):
        down, across = CHUNK // 16, half // 128
        return (
            r // (down * across),
            pl.ds(pl.multiple_of(lax.rem(r, down) * 16, 16), 16),
            pl.ds(pl.multiple_of(lax.rem(r // down, across) * 128, 128), 128),
        )

    def place_of(a, r):
        return packed.at[count_tile(r)] if a == COUNT else land.at[a, r]

    def remote(src, dst, sems, to):
        return pltpu.make_async_remote_copy(
            src_ref=src, dst_ref=dst, send_sem=sems[0], recv_sem=sems[1], device_id=to, device_id_type=MESH
        )

    def plane(a, i, cc):
        target = partner(i)
        src = tell.at[target] if a == COUNT else picked[a].at[target, cc]
        return remote(src, place_of(a, rank(i, y, c)), (in_sem.at[a, 0, i, cc], in_sem.at[a, 1, i, c]), (target, 2 * y + cc))

    def landed(a, i, cc):
        ref = place_of(a, rank(i, y, cc))
        return remote(ref, ref, (in_sem.at[a, 0, i, cc], in_sem.at[a, 1, i, cc]), (me, over_y))

    def forward(a, i, cc):
        ref = place_of(a, rank(i, y, cc))
        return remote(ref, ref, (in_sem.at[a, 2, i, cc], in_sem.at[a, 3, i, cc]), (me, over_y))

    def forward_own(a):
        src = tell.at[me] if a == COUNT else picked[a].at[me, c]
        return remote(src, place_of(a, rank(0, y, c)), (in_sem.at[a, 2, 0, c], in_sem.at[a, 3, 0, c]), (me, over_y))

    def forwarded(a, i, cc):
        ref = place_of(a, rank(i, 1 - y, cc))
        return remote(ref, ref, (in_sem.at[a, 2, i, cc], in_sem.at[a, 3, i, cc]), (me, over_y))

    def keep_own(a):
        return pltpu.make_async_copy(picked[a].at[me, c], land.at[a, rank(0, y, c)], local_sem.at[a])

    def over_peers(body, first=0):
        def step(i, carry):
            for cc in range(2):

                @pl.when(jnp.logical_or(i > 0, cc != c))
                def _():
                    body(i, cc)

            return carry

        lax.fori_loop(first, experts, step, 0)

    token = lax.broadcasted_iota(jnp.int32, (capp, 128), 1)

    def count(target):
        load = jnp.sum(jnp.where(slots[target] < toks, 1.0, 0.0), axis=0, keepdims=True)
        tell[target] = jnp.broadcast_to(load, (16, 128)).astype(BF16)

    def pick(a, target):
        where = slots[target]
        hot = jnp.concatenate([jnp.where(where == token + 128 * t, 1.0, 0.0).astype(BF16) for t in range(toks // 128)], axis=1)
        block = dot(hot, ubuf[a, :pieces].reshape(toks, width)).astype(BF16)
        picked[a][target, 0] = block[:, :half]
        picked[a][target, 1] = block[:, half:]

    def count_all(i, carry):
        count(i)
        return carry

    lax.fori_loop(0, experts, count_all, 0)
    packed[count_tile(rank(0, y, c))] = tell[me]
    for copy in load_rows[:pieces]:
        copy.wait()
    pick(X, me)
    pl.semaphore_wait(barrier, 2 * experts + 1)
    over_peers(lambda i, cc: plane(COUNT, i, cc).start())
    forward_own(COUNT).start()
    plane(X, 0, 1 - c).start()
    forward_own(X).start()
    keep_own(X).start()

    def send_out(a):
        def body(i, carry):
            pick(a, partner(i))
            plane(a, i, 0).start()
            plane(a, i, 1).start()
            return carry

        lax.fori_loop(1, experts, body, 0)

    def pass_on(a, i, cc):
        landed(a, i, cc).wait_recv()
        forward(a, i, cc).start()

    send_out(X)
    over_peers(lambda i, cc: pass_on(COUNT, i, cc))
    for copy in load_rows[pieces:]:
        copy.wait()
    pick(G, me)
    plane(G, 0, 1 - c).start()
    forward_own(G).start()
    keep_own(G).start()
    send_out(G)

    def await_count(i, carry):
        for cc in range(2):
            forwarded(COUNT, i, cc).wait_recv()
        return carry

    lax.fori_loop(0, experts, await_count, 0)

    def table(r, start):
        load = packed[count_tile(r)][0:8, :].astype(F32)[0:1, :].astype(jnp.int32)
        starts[pl.ds(r, 1)] = start
        loads[pl.ds(r, 1)] = load
        return start + load

    lax.fori_loop(0, blocks, table, jnp.zeros((1, 128), jnp.int32))

    def packed_place(low, n):
        slot = lax.broadcasted_iota(jnp.int32, (n, capp, 128), 1)
        where = jnp.where(slot < loads[pl.ds(low, n)][:, None, :], slot + starts[pl.ds(low, n)][:, None, :], -1)
        return where.reshape(n * capp, 128)

    def pass_some(a, low, high):
        def step(i, carry):
            for cc in range(2):

                @pl.when(jnp.logical_or(i > 0, cc != c))
                def _():
                    pass_on(a, i, cc)

            return carry

        lax.fori_loop(low, high, step, 0)

    windows = [row_window(k, blocks, cap, rows) for k in range(chunks)]

    def fetch_copy(a, k):
        low, high = windows[k]
        return pltpu.make_async_copy(land.at[a, pl.ds(low, high - low)], window.at[pl.ds(0, high - low)], local_sem.at[2])

    def fetch(a, k):
        before = -(-windows[k - 1][1] // 4) if k else 0

        def body(i, carry):
            for cc in range(2):
                forwarded(a, i, cc).wait_recv()
            return carry

        lax.fori_loop(before, -(-windows[k][1] // 4), body, 0)
        fetch_copy(a, k).start()

    def half_core(a, k, part):
        ref = (xbuf, gbuf)[a].at[lax.rem(k, 3), :, pl.ds(pl.multiple_of(part * half, half), half)]
        return remote(ref, ref, (half_sem.at[a, 0, k], half_sem.at[a, 1, k]), (me, over_c))

    def pack(a, k):
        low, high = windows[k]
        where = packed_place(low, high - low)
        number = lax.broadcasted_iota(jnp.int32, where.shape, 1) + k * CHUNK
        hot = jnp.concatenate([jnp.where(where == number + 128 * t, 1.0, 0.0).astype(BF16) for t in range(CHUNK // 128)], axis=1)
        fetch_copy(a, k).wait()
        block = dot_tn(hot, window[: high - low].reshape((high - low) * capp, half))
        (xbuf, gbuf)[a][k % 3, :, own_cols] = block.astype(BF16)
        half_core(a, k, c).start()

    STEP = 32

    def over_rows(count, body):
        def step(i, carry):
            body(pl.multiple_of(i * STEP, STEP))
            return carry

        lax.fori_loop(0, count // STEP, step, 0, unroll=4)

    def row_stats(v):
        mean = jnp.mean(v, axis=-1, keepdims=True)
        v = v - mean
        scale = lax.rsqrt(jnp.mean(v * v, axis=-1, keepdims=True) + EPS)
        return v * scale, scale

    def tiles(n):
        return [slice(t * 256, (t + 1) * 256) for t in range(n // 256)]

    def first(layer, normed, slot):
        for f in tiles(hidden):
            a = dot(normed(), wbuf[layer, 0, :, f]) + b_in[layer : layer + 1, f]
            sq = a * a
            t = jnp.tanh(a * (C1 + (C1 * C2) * sq))
            up = 0.5 + 0.5 * t
            ubuf[slot, 1, :, f] = (a * up).astype(BF16)
            ubuf[slot, 0, :, f] = (up + (0.5 * a) * (1.0 - t * t) * (C1 + (3.0 * C1 * C2) * sq)).astype(BF16)

    def second(layer, slot):
        for d in tiles(width):
            pscr[:, d] = dot(ubuf[slot, 1], wbuf[layer, 1, :, d])

    def back(layer, grad, slot, into):
        for f in tiles(hidden):
            da = (dot_nt(grad(), wbuf[layer, 1, f, :]) * ubuf[slot, 0, :, f].astype(F32)).astype(BF16)
            into[:, f] = da
            btally[layer, :, f] += fold(da.astype(F32))
        for d in tiles(width):
            pscr[:, d] = dot_nt(into[...], wbuf[layer, 0, d, :])

    def weight_grads(normed, grad, active, before):
        for f in tiles(hidden):
            acc_out[f, :] += dot_tn(active(f), grad())
        for d in tiles(width):
            acc_in[d, :] += dot_tn(normed(d), before())

    def split_rows(k, ring):
        own[ring] = pscr[own_rows]
        csend[ring] = pscr[other_rows].astype(BF16)

    def split_cols(ring):
        mown[...] = pscr[:, own_cols]
        msend[ring] = pscr[:, other_cols].astype(BF16)

    def fold(value):
        return jnp.sum(value.reshape(value.shape[0] // 8, 8, value.shape[1]), axis=0)

    def add_row(row, value):
        tally[row] += fold(value)

    GAIN0, GAIN1, SHIFT0, SHIFT1, BOUT0, BOUT1, CENT = range(7)

    def stage_a(k):
        ring, slot = lax.rem(k, 2), lax.rem(k, 3)
        half_core(X, k, 1 - c).wait_recv()
        save_x(k).start()

        def body(r):
            v = xbuf[slot, pl.ds(r, STEP)].astype(F32)
            share = jax.nn.sigmoid(jnp.sum(v * center[...], axis=-1, keepdims=True))
            stat[k, pl.ds(r, STEP), 0:1] = share
            unit, _ = row_stats(v)
            ubuf[ring, 2, pl.ds(r, STEP)] = (unit * gains[0:1] + shifts[0:1]).astype(BF16)


        @pl.when(k >= 2)
        def _():
            save_u(k - 2).wait()
            p_core(k - 2).wait_send()

        over_rows(CHUNK, body)
        first(0, lambda: ubuf[ring, 2], ring)
        save_u(k).start()
        second(0, ring)
        split_rows(k, ring)
        save_x(k).wait()
        half_core(X, k, c).wait_send()
        p_core(k).start()

    def stage_sum(k, core, over, which):
        core(k).wait_recv()
        ysend[which, k] = (own[lax.rem(k, 2)] + crecv[lax.rem(k, 4)].astype(F32)).astype(BF16)
        over(k).start()

    def loop1(k, carry):
        for i in range(1, chunks):

            @pl.when(k == i - 1)
            def _():
                pack(X, i)
                if i + 1 < chunks:
                    fetch(X, i + 1)

        @pl.when(k < chunks)
        def _():
            pass_some(G, k * (experts // chunks), (k + 1) * (experts // chunks))
            stage_a(k)

        @pl.when(k >= 1)
        def _():
            stage_sum(k - 1, p_core, p_y, 0)

        return carry

    for copy in load_w(0):
        copy.wait()
    keep_own(X).wait()
    keep_own(G).wait()
    first_need = -(-windows[0][1] // 4)
    pass_some(X, 0, first_need)
    fetch(X, 0)
    pass_some(X, first_need, experts)
    pack(X, 0)
    fetch(X, 1)
    lax.fori_loop(0, chunks + 1, loop1, 0)
    for k in (chunks - 2, chunks - 1):
        save_u(k).wait()
        p_core(k).wait_send()
    load_x(0).start()
    fetch(G, 0)
    pack(G, 0)
    over_peers(lambda i, cc: plane(X, i, cc).wait_send())
    over_peers(lambda i, cc: plane(G, i, cc).wait_send())
    over_peers(lambda i, cc: forward(COUNT, i, cc).wait_send())
    for a in range(3):
        forward_own(a).wait_send()
    for copy in load_w(1):
        copy.wait()

    def stage_c(k):
        ring, slot = lax.rem(k, 2), lax.rem(k, 3)
        p_y(k).wait_recv()
        half_core(G, k, 1 - c).wait_recv()

        def body(r):
            here = pl.ds(r, STEP)
            there = pl.ds(pl.multiple_of(c * side + r, STEP), STEP)
            x = xbuf[slot, there].astype(F32)
            g = gbuf[slot, there].astype(F32)
            share = stat[k, there, 0:1]
            state = x + (ysend[0, k, here].astype(F32) + yrecv[0, k, here].astype(F32)) + b_out[0:1]
            unit, scale = row_stats(state)
            unit1[k, here] = unit.astype(BF16)
            stat[k, there, 2:3] = scale
            nbuf[k, c, here] = (unit * gains[1:2] + shifts[1:2]).astype(BF16)
            diff = state + b_out[1:2] - x
            base[ring, here] = 0.5 * (share * diff + x)
            pull = jnp.sum(g * diff, axis=-1, keepdims=True)
            stat[k, there, 1:2] = 0.5 * share * (1.0 - share) * pull

        over_rows(side, body)
        n_core(k, c).start()
        stat[k, other_rows, 1:2] = jnp.zeros((side, 1), F32)

    def stage_d(k):
        ring, slot = lax.rem(k, 2), lax.rem(k, 3)
        n_core(k, 1 - c).wait_recv()
        save_g(k).start()
        normed = lambda: nbuf[k].reshape(CHUNK, width)
        first(1, normed, 0)
        second(1, 0)

        def body(r, based):
            at = (c if based else 1 - c) * side + r
            there = pl.ds(pl.multiple_of(at, STEP), STEP)
            g = gbuf[slot, there].astype(F32)
            share = stat[k, there, 0:1]
            p = pscr[there]
            pull = jnp.sum(g * p, axis=-1, keepdims=True)
            stat[k, there, 1:2] = stat[k, there, 1:2] + share * (1.0 - share) * pull
            out = share * p
            if based:
                out = out + base[ring, pl.ds(r, STEP)]
            pscr[there] = out
            grad = share * g
            nscr[there] = grad.astype(BF16)
            add_row(BOUT1, 0.25 * grad)

        over_rows(side, functools.partial(body, based=True))
        over_rows(side, functools.partial(body, based=False))

        @pl.when(k >= 2)
        def _():
            m_core(k - 2).wait_send()
            d_core(k - 2).wait_send()

        split_cols(ring)
        m_core(k).start()
        back(1, lambda: nscr[...], 0, ascr)
        split_rows(k, ring)
        save_g(k).wait()
        half_core(G, k, c).wait_send()
        d_core(k).start()
        weight_grads(lambda d: nbuf[k, :, :, d].reshape(CHUNK, 256), lambda: nscr[...], lambda f: ubuf[0, 1, :, f], lambda: ascr[...])

    def stage_pack(k, core):
        core(k).wait_recv()
        packed[k] = (mown[...] + mrecv[lax.rem(k, 4)].astype(F32)).astype(BF16)

    def group_copy(a, g):
        part = pl.ds(g * span, span)
        return pltpu.make_async_remote_copy(
            src_ref=esend.at[part],
            dst_ref=erecv.at[a, part],
            send_sem=group_sem.at[a, 0, g],
            recv_sem=group_sem.at[a, 1, g],
            device_id=(me, over_y),
            device_id_type=MESH,
        )

    def plane_copy(a, d, cc):
        target = partner(d)
        return pltpu.make_async_remote_copy(
            src_ref=eown.at[d, cc],
            dst_ref=back_rows.at[a, c, me],
            send_sem=plane_sem.at[a, 0, d, cc],
            recv_sem=plane_sem.at[a, 1, d, c],
            device_id=(target, 2 * y + cc),
            device_id_type=MESH,
        )

    def plane_landed(a, d, cc):
        source = partner(d)
        ref = back_rows.at[a, cc, source]
        return pltpu.make_async_remote_copy(
            src_ref=ref,
            dst_ref=ref,
            send_sem=plane_sem.at[a, 0, d, cc],
            recv_sem=plane_sem.at[a, 1, d, cc],
            device_id=(me, over_y),
            device_id_type=MESH,
        )

    def group_rows(g):
        low = max(0, rows - cap * blocks + cap * 4 * g * span) // CHUNK
        high = min(chunks, -(-(cap * 4 * (g + 1) * span) // CHUNK))
        return low, high

    def expand(g, a):
        low, high = group_rows(g)
        if a:
            group_copy(0, g).wait_send()
        number = lax.broadcasted_iota(jnp.int32, (2 * capp, 128), 1) + low * CHUNK

        def part(i, yy, into):
            where = packed_place(4 * (g * span + i) + 2 * yy, 2)
            hot = jnp.concatenate(
                [jnp.where(where == number + 128 * t, 1.0, 0.0).astype(BF16) for t in range((high - low) * CHUNK // 128)], axis=1
            )
            block = dot(hot, packed[low:high].reshape((high - low) * CHUNK, half))
            into[g * span + i] = block.astype(BF16).reshape(2, capp, half)

        def far(i, carry):
            part(i, 1 - y, esend)
            return carry

        def near(i, carry):
            if a:
                finish(0, g * span + i)
            part(i, y, eown)
            return carry

        lax.fori_loop(0, span, far, 0, unroll=2)
        group_copy(a, g).start()
        lax.fori_loop(0, span, near, 0, unroll=2)

    def self_copy(a):
        return pltpu.make_async_copy(eown.at[0, c], back_rows.at[a, c, me], local_sem.at[1])

    def finish(a, d):
        @pl.when(d > 0)
        def _():
            plane_copy(a, d, 0).wait_send()
            plane_copy(a, d, 1).wait_send()

        @pl.when(d == 0)
        def _():
            plane_copy(a, 0, 1 - c).wait_send()
            self_copy(a).wait()

    def give_back(a, g):
        group_copy(a, g).wait_recv()

        def one(i, carry):
            d = g * span + i
            eown[d] = (eown[d].astype(F32) + erecv[a, d].astype(F32)).astype(BF16)

            @pl.when(d > 0)
            def _():
                plane_copy(a, d, 0).start()
                plane_copy(a, d, 1).start()

            @pl.when(d == 0)
            def _():
                plane_copy(a, 0, 1 - c).start()
                self_copy(a).start()

            return carry

        lax.fori_loop(0, span, one, 0)

    ready = [group_rows(g)[1] for g in range(groups)]

    def loop2(k, carry):
        @pl.when(k < chunks)
        def _():
            load_x(k).wait()

        @pl.when(k + 1 < chunks)
        def _():
            load_x(k + 1).start()

        @pl.when(k >= 2)
        def _():
            stage_sum(k - 2, d_core, d_y, 1)

        for i in range(1, chunks):

            @pl.when(k == i - 1)
            def _():
                fetch(G, i)

        @pl.when(k < chunks)
        def _():
            stage_c(k)

        for i in range(1, chunks):

            @pl.when(k == i - 1)
            def _():
                pack(G, i)

        @pl.when(k >= 2)
        def _():
            stage_pack(k - 2, m_core)

        for g in range(groups):
            if ready[g] < chunks:

                @pl.when(k - 1 == ready[g])
                def _():
                    expand(g, 0)

        @pl.when(jnp.logical_and(k >= 1, k <= chunks))
        def _():
            stage_d(k - 1)

        return carry

    lax.fori_loop(0, chunks + 2, loop2, 0)
    for k in (chunks - 2, chunks - 1):
        m_core(k).wait_send()
        d_core(k).wait_send()

    def save_grads(layer):
        return pltpu.make_async_copy(wbuf.at[layer], gw.at[layer], w_sem.at[layer, 0])

    def round_grads(layer, wipe):
        def body(i, carry):
            rng = pl.ds(pl.multiple_of(i * 32, 32), 32)
            wbuf[layer, 0, rng] = acc_in[rng].astype(BF16)
            wbuf[layer, 1, rng] = acc_out[rng].astype(BF16)
            if wipe:
                acc_in[rng] = jnp.zeros((32, hidden), F32)
                acc_out[rng] = jnp.zeros((32, width), F32)
            return carry

        lax.fori_loop(0, width // 32, body, 0)

    round_grads(1, True)
    save_grads(1).start()
    load_x(0).start()
    load_g(0).start()
    load_u(0).start()
    for g in range(groups):
        if ready[g] >= chunks:
            expand(g, 0)
    save_grads(1).wait()

    def stage_g(k):
        ring, slot = lax.rem(k, 2), lax.rem(k, 3)
        d_y(k).wait_recv()
        n_core(k, c).wait_send()

        def body(r):
            here = pl.ds(r, STEP)
            there = pl.ds(pl.multiple_of(c * side + r, STEP), STEP)
            g = gbuf[slot, there].astype(F32)
            share = stat[k, there, 0:1]
            dn = ysend[1, k, here].astype(F32) + yrecv[1, k, here].astype(F32)
            unit = unit1[k, here].astype(F32)
            w = dn * gains[1:2]
            add_row(GAIN1, 0.5 * dn * unit)
            add_row(SHIFT1, 0.5 * dn)
            grad = share * g + stat[k, there, 2:3] * (
                w - jnp.mean(w, axis=-1, keepdims=True) - unit * jnp.mean(w * unit, axis=-1, keepdims=True)
            )
            nbuf[k, c, here] = grad.astype(BF16)
            add_row(BOUT0, 0.5 * grad)
            base[ring, here] = 0.5 * (grad + (1.0 - share) * g)

        over_rows(side, body)
        dp_core(k, c).start()

    def before_at(k):
        per = chunks // 2
        return wbuf.at[1, k // per, pl.ds(pl.multiple_of(lax.rem(k, per) * CHUNK, CHUNK), CHUNK)]

    def stage_h(k):
        ring, slot = lax.rem(k, 2), lax.rem(k, 3)
        dp_core(k, 1 - c).wait_recv()
        back(0, lambda: nbuf[k].reshape(CHUNK, width), ring, before_at(k))

        def body(r, based):
            at = (c if based else 1 - c) * side + r
            there = pl.ds(pl.multiple_of(at, STEP), STEP)
            x = xbuf[slot, there].astype(F32)
            pull = stat[k, there, 1:2]
            unit, scale = row_stats(x)
            dn = pscr[there]
            w = dn * gains[0:1]
            add_row(GAIN0, dn * unit)
            add_row(SHIFT0, dn)
            add_row(CENT, pull * x)
            out = pull * center[...] + scale * (
                w - jnp.mean(w, axis=-1, keepdims=True) - unit * jnp.mean(w * unit, axis=-1, keepdims=True)
            )
            if based:
                out = out + base[ring, pl.ds(r, STEP)]
            pscr[there] = out

        over_rows(side, functools.partial(body, based=True))
        over_rows(side, functools.partial(body, based=False))

        @pl.when(k >= 2)
        def _():
            z_core(k - 2).wait_send()

        split_cols(ring)
        z_core(k).start()

    def stage_w(k, carry):
        load_un(k).wait()

        @pl.when(k + 1 < chunks)
        def _():
            load_un(k + 1).start()

        slot = lax.rem(k, 2)
        weight_grads(
            lambda d: ubuf[slot, 2, :, d],
            lambda: nbuf[k].reshape(CHUNK, width),
            lambda f: ubuf[slot, 1, :, f],
            lambda: before_at(k)[...],
        )
        return carry

    def loop3(k, carry):
        @pl.when(k < chunks)
        def _():
            load_x(k).wait()
            load_g(k).wait()

        @pl.when(k + 1 < chunks)
        def _():
            load_x(k + 1).start()
            load_g(k + 1).start()

        @pl.when(k >= 2)
        def _():
            stage_pack(k - 2, z_core)

        @pl.when(k < chunks)
        def _():
            stage_g(k)

        @pl.when(k >= 1)
        def _():
            load_u(k - 1).wait()

        @pl.when(jnp.logical_and(k >= 1, k < chunks))
        def _():
            load_u(k).start()

        @pl.when(k >= 1)
        def _():
            stage_h(k - 1)

        for g in range(groups):

            @pl.when(k == 1 + g * (chunks // groups))
            def _():
                give_back(0, g)

        for g in range(groups):
            if ready[g] < chunks:

                @pl.when(k - 1 == ready[g])
                def _():
                    expand(g, 1)

        return carry

    lax.fori_loop(0, chunks + 1, loop3, 0)
    stage_pack(chunks - 1, z_core)
    for g in range(groups):
        if ready[g] >= chunks:
            expand(g, 1)
    load_un(0).start()

    for row in range(8):
        mine[row : row + 1] = jnp.sum(tally[row], axis=0, keepdims=True)
    for layer in range(SUBLAYERS):
        gb_in[layer : layer + 1] = jnp.sum(btally[layer], axis=0, keepdims=True)
    tallies[place] = mine[...]

    def tally_copy(i, to):
        return pltpu.make_async_remote_copy(
            src_ref=mine,
            dst_ref=tallies.at[place],
            send_sem=sum_sem.at[0, i],
            recv_sem=sum_sem.at[1, i],
            device_id=(me, to),
            device_id_type=MESH,
        )

    def tally_landed(i, frm):
        ref = tallies.at[frm]
        return pltpu.make_async_remote_copy(
            src_ref=ref, dst_ref=ref, send_sem=sum_sem.at[0, i], recv_sem=sum_sem.at[1, i], device_id=(me, frm), device_id_type=MESH
        )

    others = (over_c, over_y, over_both)
    for i, to in enumerate(others):
        tally_copy(i, to).start()
    for g in range(groups // 2):
        give_back(1, g)
    lax.fori_loop(0, chunks, stage_w, 0)
    round_grads(0, False)
    save_grads(0).start()
    for g in range(groups // 2, groups):
        give_back(1, g)

    def gather_back(a, result):
        def wait(d, carry):
            for cc in range(2):

                @pl.when(jnp.logical_or(d > 0, cc != c))
                def _():
                    plane_landed(a, d, cc).wait_recv()

            return carry

        lax.fori_loop(0, experts, wait, 0)
        if a:
            self_copy(1).wait()
        lane = lax.broadcasted_iota(jnp.int32, (experts * capp, 128), 1)
        where = slots[...].reshape(experts * capp, 128)
        for j in range(2):
            copy = pltpu.make_async_copy(back_rows.at[a, j], window.at[pl.ds(0, experts)], local_sem.at[0])
            copy.start()
            copy.wait()
            for i, hold in enumerate((nscr, ascr)):
                hot = jnp.concatenate(
                    [jnp.where(where == lane + (i * CHUNK + 128 * t), 1.0, 0.0).astype(BF16) for t in range(CHUNK // 128)], axis=1
                )
                block = window[:experts]
                hold[:, j * half : (j + 1) * half] = dot_tn(hot, block.reshape(experts * capp, half)).astype(BF16)
        for i, hold in enumerate((nscr, ascr)):
            pltpu.make_async_copy(hold, result.at[pl.ds(i * CHUNK, CHUNK)], local_sem.at[2 + i]).start()

    def gathered(result):
        for i, hold in enumerate((nscr, ascr)):
            pltpu.make_async_copy(hold, result.at[pl.ds(i * CHUNK, CHUNK)], local_sem.at[2 + i]).wait()

    gather_back(0, mixed)
    for i, frm in enumerate(others):
        tally_landed(i, frm).wait_recv()
        tally_copy(i, frm).wait_send()
    sums[...] = (tallies[0] + tallies[1]) + (tallies[2] + tallies[3])
    gathered(mixed)
    gather_back(1, gtok)
    for g in range(groups):
        group_copy(1, g).wait_send()

    def last(d, carry):
        @pl.when(d > 0)
        def _():
            plane_copy(1, d, 0).wait_send()
            plane_copy(1, d, 1).wait_send()

        @pl.when(d == 0)
        def _():
            plane_copy(1, 0, 1 - c).wait_send()

        return carry

    lax.fori_loop(0, experts, last, 0)

    over_peers(lambda i, cc: plane(COUNT, i, cc).wait_send())
    for a in (X, G):
        over_peers(lambda i, cc: forward(a, i, cc).wait_send())

    def last_chunk(k, carry):
        p_y(k).wait_send()
        d_y(k).wait_send()
        dp_core(k, c).wait_send()
        return carry

    lax.fori_loop(0, chunks, last_chunk, 0)
    for k in (chunks - 2, chunks - 1):
        z_core(k).wait_send()
    save_grads(0).wait()
    gathered(gtok)


def layers(cap, slots, tok, cot, w_in, w_out, b_in, b_out, gains, shifts, center):
    experts, capp = slots.shape[:2]
    blocks = 4 * experts
    toks, width = tok.shape
    rows = 4 * toks
    hidden = b_in.shape[1]
    half, side, chunks = width // 2, CHUNK // 2, rows // CHUNK
    span = experts // GROUPS
    windows = [row_window(k, blocks, cap, rows) for k in range(chunks)]
    reach = max(high - low for low, high in windows)
    vmem = pl.BlockSpec(memory_space=pltpu.VMEM)
    hbm = pl.BlockSpec(memory_space=pl.ANY)
    dma = pltpu.SemaphoreType.DMA
    return pl.pallas_call(
        functools.partial(layers_kernel, experts, cap),
        out_shape=(
            jax.ShapeDtypeStruct((toks, width), BF16),
            jax.ShapeDtypeStruct((toks, width), BF16),
            jax.ShapeDtypeStruct((SUBLAYERS, 2, width, width), BF16),
            jax.ShapeDtypeStruct((SUBLAYERS, hidden), F32),
            jax.ShapeDtypeStruct((8, width), F32),
            jax.ShapeDtypeStruct((chunks, 3, CHUNK, hidden), BF16),
            jax.ShapeDtypeStruct((2, 2, experts, capp, half), BF16),
            jax.ShapeDtypeStruct((2, blocks, capp, half), BF16),
            jax.ShapeDtypeStruct((rows, width), BF16),
            jax.ShapeDtypeStruct((rows, width), BF16),
        ),
        in_specs=[vmem, hbm, hbm, hbm, hbm, vmem, vmem, vmem, vmem, vmem],
        out_specs=(hbm, hbm, hbm, vmem, vmem, hbm, hbm, hbm, hbm, hbm),
        scratch_shapes=[
            pltpu.VMEM((SUBLAYERS, 2, width, width), BF16),
            pltpu.VMEM((width, hidden), F32),
            pltpu.VMEM((hidden, width), F32),
            pltpu.VMEM((3, CHUNK, width), BF16),
            pltpu.VMEM((3, CHUNK, width), BF16),
            pltpu.VMEM((reach, capp, half), BF16),
            pltpu.VMEM((blocks, 128), jnp.int32),
            pltpu.VMEM((blocks, 128), jnp.int32),
            pltpu.VMEM((experts, 16, 128), BF16),
            pltpu.VMEM((2, 3, CHUNK, hidden), BF16),
            pltpu.VMEM((chunks, 2, side, width), BF16),
            pltpu.VMEM((CHUNK, width), BF16),
            pltpu.VMEM((CHUNK, hidden), BF16),
            pltpu.VMEM((CHUNK, width), F32),
            pltpu.VMEM((2, side, width), F32),
            pltpu.VMEM((2, side, width), BF16),
            pltpu.VMEM((4, side, width), BF16),
            pltpu.VMEM((2, chunks, side, width), BF16),
            pltpu.VMEM((2, chunks, side, width), BF16),
            pltpu.VMEM((chunks, side, width), BF16),
            pltpu.VMEM((2, side, width), F32),
            pltpu.VMEM((chunks, CHUNK, 128), F32),
            pltpu.VMEM((CHUNK, half), F32),
            pltpu.VMEM((2, CHUNK, half), BF16),
            pltpu.VMEM((4, CHUNK, half), BF16),
            pltpu.VMEM((chunks, CHUNK, half), BF16),
            pltpu.VMEM((experts, 2, capp, half), BF16),
            pltpu.VMEM((experts, 2, capp, half), BF16),
            pltpu.VMEM((2, experts, 2, capp, half), BF16),
            pltpu.VMEM((8, 8, width), F32),
            pltpu.VMEM((SUBLAYERS, 8, hidden), F32),
            pltpu.VMEM((8, width), F32),
            pltpu.VMEM((4, 8, width), F32),
            dma((8, 2, chunks)),
            dma((2, 2, GROUPS)),
            dma((2, 2, experts, 2)),
            dma((2, 3)),
            dma((SUBLAYERS, 2)),
            dma((3,)),
            dma((3,)),
            dma((2, 2)),
            dma((4,)),
            dma((3, 4, experts, 2)),
            dma((2, 2, chunks)),
        ],
        compiler_params=pltpu.CompilerParams(collective_id=0, has_side_effects=True, vmem_limit_bytes=62 * 2**20),
        name="layers",
    )(slots, tok, cot, w_in, w_out, b_in, b_out, gains, shifts, center)


def on_device(experts, places, tokens, dispatch_rows, w_in, w_out, b_in, b_out, ln_gain, ln_bias, centroid, cotangent):
    slots = dispatch_rows[0]
    toks = tokens.shape[0]
    cap = slots.shape[1]
    capp = -(-cap // 16) * 16
    padded = jnp.pad(slots, ((0, 0), (0, capp - cap)), constant_values=toks)
    spread = jnp.broadcast_to(padded[:, :, None], (experts, capp, 128))
    mixed, gtok, gw, gb_in, sums = layers(
        cap, spread, tokens, cotangent, w_in[0], w_out[0], b_in[0], b_out[0], ln_gain[0], ln_bias[0], centroid
    )[:5]
    return (
        mixed,
        gtok.astype(F32),
        gw[None, :, 0].astype(F32),
        gw[None, :, 1].astype(F32),
        gb_in[None],
        sums[None, 4:6],
        sums[None, 0:2],
        sums[None, 2:4],
        sums[6:7],
    )


def solution(mesh):
    rows = P(("expert", "hidden"), None)
    return jax.shard_map(
        functools.partial(on_device, mesh.shape["expert"], mesh.shape["hidden"]),
        mesh=mesh,
        in_specs=(
            rows,
            P(("expert", "hidden"), None, None),
            P("expert", None, None, "hidden"),
            P("expert", None, "hidden", None),
            P("expert", None, "hidden"),
            P("expert", None, None),
            P("expert", None, None),
            P("expert", None, None),
            P("expert", None),
            rows,
        ),
        out_specs=(
            rows,
            rows,
            P("expert", None, None, "hidden"),
            P("expert", None, "hidden", None),
            P("expert", None, "hidden"),
            P("expert", None, None),
            P("expert", None, None),
            P("expert", None, None),
            P("expert", None),
        ),
        check_vma=False,
    )
```

```python
import functools

import jax
import jax.numpy as jnp
from jax import lax
from jax.experimental import pallas as pl
from jax.experimental.pallas import tpu as pltpu
from jax.sharding import PartitionSpec as P

MESH = pl.DeviceIdType.MESH
SUBLAYERS = 2
EPS = 1e-05
F32 = jnp.float32
BF16 = jnp.bfloat16
CHUNK = 256
GROUPS = 8
C1 = 0.7978845608028654
C2 = 0.044715


def dot(left, right):
    return jnp.dot(left, right, preferred_element_type=F32)


def dot_tn(left, right):
    return lax.dot_general(left, right, (((0,), (0,)), ((), ())), preferred_element_type=F32)


def dot_nt(left, right):
    return lax.dot_general(left, right, (((1,), (1,)), ((), ())), preferred_element_type=F32)


def row_window(chunk, blocks, cap, rows):
    low = (chunk * CHUNK) // cap
    high = min(blocks - 1, (chunk * CHUNK + CHUNK - 1 + cap * blocks - rows) // cap)
    return low, high + 1


def layers_kernel(
    experts,
    cap,
    slots, tok, cot, w_in, w_out, b_in, b_out, gains, shifts, center,
    mixed, gtok, gw, gb_in, sums, spill, back_rows, land, xc, gc,
    wbuf, acc_in, acc_out, xbuf, gbuf, window, starts, loads, tell, ubuf, nbuf, nscr, ascr, pscr, own, csend, crecv,
    ysend, yrecv, unit1, base, stat, mown, msend, mrecv, packed, esend, eown, erecv, tally, btally, mine, tallies,
    chunk_sem, group_sem, plane_sem, sum_sem, w_sem, x_sem, g_sem, u_sem, local_sem, in_sem, half_sem,
):
    me = lax.axis_index("expert")
    place = lax.axis_index("hidden")
    y = place // 2
    c = lax.rem(place, 2)
    over_y = lax.rem(place + 2, 4)
    over_c = place + 1 - 2 * c
    over_both = 3 - place
    rows, width = xc.shape
    chunks = rows // CHUNK
    hidden = b_in.shape[1]
    half = width // 2
    side = CHUNK // 2
    toks = mixed.shape[0]
    capp = slots.shape[1]
    blocks = 4 * experts
    groups = GROUPS
    span = experts // groups

    barrier = pltpu.get_barrier_semaphore()

    def greet(i, carry):
        e = lax.rem(me + i // 2, experts)
        cc = lax.rem(i, 2)

        @pl.when(jnp.logical_or(i // 2 > 0, cc != c))
        def _():
            pl.semaphore_signal(barrier, 1, device_id=(e, 2 * y + cc), device_id_type=MESH)

        return carry

    lax.fori_loop(0, 2 * experts, greet, 0)
    pl.semaphore_signal(barrier, 1, device_id=(me, over_y), device_id_type=MESH)
    pl.semaphore_signal(barrier, 1, device_id=(me, over_both), device_id_type=MESH)

    own_rows = pl.ds(pl.multiple_of(c * side, side), side)
    other_rows = pl.ds(pl.multiple_of((1 - c) * side, side), side)
    own_cols = pl.ds(pl.multiple_of(c * half, half), half)
    other_cols = pl.ds(pl.multiple_of((1 - c) * half, half), half)

    def send(src, dst, kind, k, to):
        return pltpu.make_async_remote_copy(
            src_ref=src,
            dst_ref=dst,
            send_sem=chunk_sem.at[kind, 0, k],
            recv_sem=chunk_sem.at[kind, 1, k],
            device_id=(me, to),
            device_id_type=MESH,
        )

    P_CORE, P_Y, N_CORE, M_CORE, D_CORE, D_Y, DP_CORE, Z_CORE = range(8)

    def p_core(k):
        return send(csend.at[lax.rem(k, 2)], crecv.at[lax.rem(k, 4)], P_CORE, k, over_c)

    def d_core(k):
        return send(csend.at[lax.rem(k, 2)], crecv.at[lax.rem(k, 4)], D_CORE, k, over_c)

    def p_y(k):
        return send(ysend.at[0, k], yrecv.at[0, k], P_Y, k, over_y)

    def d_y(k):
        return send(ysend.at[1, k], yrecv.at[1, k], D_Y, k, over_y)

    def n_core(k, part):
        return send(nbuf.at[k, part], nbuf.at[k, part], N_CORE, k, over_c)

    def dp_core(k, part):
        return send(nbuf.at[k, part], nbuf.at[k, part], DP_CORE, k, over_c)

    def m_core(k):
        return send(msend.at[lax.rem(k, 2)], mrecv.at[lax.rem(k, 4)], M_CORE, k, over_c)

    def z_core(k):
        return send(msend.at[lax.rem(k, 2)], mrecv.at[lax.rem(k, 4)], Z_CORE, k, over_c)

    def load_x(k):
        return pltpu.make_async_copy(xc.at[pl.ds(k * CHUNK, CHUNK)], xbuf.at[lax.rem(k, 3)], x_sem.at[lax.rem(k, 3)])

    def load_g(k):
        return pltpu.make_async_copy(gc.at[pl.ds(k * CHUNK, CHUNK)], gbuf.at[lax.rem(k, 3)], g_sem.at[lax.rem(k, 3)])

    def save_g(k):
        return pltpu.make_async_copy(gbuf.at[lax.rem(k, 3)], gc.at[pl.ds(k * CHUNK, CHUNK)], g_sem.at[lax.rem(k, 3)])

    def save_x(k):
        return pltpu.make_async_copy(xbuf.at[lax.rem(k, 3)], xc.at[pl.ds(k * CHUNK, CHUNK)], x_sem.at[lax.rem(k, 3)])

    def save_u(k):
        return pltpu.make_async_copy(ubuf.at[lax.rem(k, 2)], spill.at[k], u_sem.at[lax.rem(k, 2), 0])

    def load_u(k):
        return pltpu.make_async_copy(spill.at[k, 0], ubuf.at[lax.rem(k, 2), 0], u_sem.at[lax.rem(k, 2), 0])

    def load_un(k):
        return pltpu.make_async_copy(spill.at[k, pl.ds(1, 2)], ubuf.at[lax.rem(k, 2), pl.ds(1, 2)], u_sem.at[lax.rem(k, 2), 0])

    def load_w(layer):
        return (
            pltpu.make_async_copy(w_in.at[layer], wbuf.at[layer, 0], w_sem.at[layer, 0]),
            pltpu.make_async_copy(w_out.at[layer], wbuf.at[layer, 1], w_sem.at[layer, 1]),
        )

    for layer in range(SUBLAYERS):
        for copy in load_w(layer):
            copy.start()
    pieces = toks // CHUNK
    load_rows = [
        pltpu.make_async_copy(ref.at[pl.ds(i * CHUNK, CHUNK)], ubuf.at[a, i], u_sem.at[a, i])
        for a, ref in enumerate((tok, cot))
        for i in range(pieces)
    ]
    for copy in load_rows:
        copy.start()
    tally[...] = jnp.zeros_like(tally)
    btally[...] = jnp.zeros_like(btally)

    def clear(acc):
        def body(i, carry):
            acc[pl.ds(pl.multiple_of(i * 32, 32), 32)] = jnp.zeros((32, acc.shape[1]), F32)
            return carry

        lax.fori_loop(0, acc.shape[0] // 32, body, 0)

    clear(acc_in)
    clear(acc_out)
    bits = experts.bit_length() - 1

    def partner(i):
        return sum(lax.rem(me // 2**j + i // 2 ** (bits - 1 - j), 2) * 2**j for j in range(bits))


    X, G, COUNT = range(3)
    picked = (esend, eown)

    def rank(i, yy, cc):
        return i * 4 + yy * 2 + cc

    def count_tile(r):
        down, across = CHUNK // 16, half // 128
        return (
            r // (down * across),
            pl.ds(pl.multiple_of(lax.rem(r, down) * 16, 16), 16),
            pl.ds(pl.multiple_of(lax.rem(r // down, across) * 128, 128), 128),
        )

    def place_of(a, r):
        return packed.at[count_tile(r)] if a == COUNT else land.at[a, r]

    def remote(src, dst, sems, to):
        return pltpu.make_async_remote_copy(
            src_ref=src, dst_ref=dst, send_sem=sems[0], recv_sem=sems[1], device_id=to, device_id_type=MESH
        )

    def plane(a, i, cc):
        target = partner(i)
        src = tell.at[target] if a == COUNT else picked[a].at[target, cc]
        return remote(src, place_of(a, rank(i, y, c)), (in_sem.at[a, 0, i, cc], in_sem.at[a, 1, i, c]), (target, 2 * y + cc))

    def landed(a, i, cc):
        ref = place_of(a, rank(i, y, cc))
        return remote(ref, ref, (in_sem.at[a, 0, i, cc], in_sem.at[a, 1, i, cc]), (me, over_y))

    def forward(a, i, cc):
        ref = place_of(a, rank(i, y, cc))
        return remote(ref, ref, (in_sem.at[a, 2, i, cc], in_sem.at[a, 3, i, cc]), (me, over_y))

    def forward_own(a):
        src = tell.at[me] if a == COUNT else picked[a].at[me, c]
        return remote(src, place_of(a, rank(0, y, c)), (in_sem.at[a, 2, 0, c], in_sem.at[a, 3, 0, c]), (me, over_y))

    def forwarded(a, i, cc):
        ref = place_of(a, rank(i, 1 - y, cc))
        return remote(ref, ref, (in_sem.at[a, 2, i, cc], in_sem.at[a, 3, i, cc]), (me, over_y))

    def keep_own(a):
        return pltpu.make_async_copy(picked[a].at[me, c], land.at[a, rank(0, y, c)], local_sem.at[a])

    def over_peers(body, first=0):
        def step(i, carry):
            for cc in range(2):

                @pl.when(jnp.logical_or(i > 0, cc != c))
                def _():
                    body(i, cc)

            return carry

        lax.fori_loop(first, experts, step, 0)

    token = lax.broadcasted_iota(jnp.int32, (capp, 128), 1)

    def count(target):
        load = jnp.sum(jnp.where(slots[target] < toks, 1.0, 0.0), axis=0, keepdims=True)
        tell[target] = jnp.broadcast_to(load, (16, 128)).astype(BF16)

    def pick(a, target):
        where = slots[target]
        hot = jnp.concatenate([jnp.where(where == token + 128 * t, 1.0, 0.0).astype(BF16) for t in range(toks // 128)], axis=1)
        block = dot(hot, ubuf[a, :pieces].reshape(toks, width)).astype(BF16)
        picked[a][target, 0] = block[:, :half]
        picked[a][target, 1] = block[:, half:]

    def count_all(i, carry):
        count(i)
        return carry

    lax.fori_loop(0, experts, count_all, 0)
    packed[count_tile(rank(0, y, c))] = tell[me]
    for copy in load_rows[:pieces]:
        copy.wait()
    pick(X, me)
    pl.semaphore_wait(barrier, 2 * experts + 1)
    over_peers(lambda i, cc: plane(COUNT, i, cc).start())
    forward_own(COUNT).start()
    plane(X, 0, 1 - c).start()
    forward_own(X).start()
    keep_own(X).start()

    def send_out(a, first, step, picking=True, sending=True):
        def body(j, carry):
            i = first + j * step
            if picking:
                pick(a, partner(i))
            if sending:
                plane(a, i, 0).start()
                plane(a, i, 1).start()
            return carry

        lax.fori_loop(0, -(-(experts - first) // step), body, 0)

    def pass_on(a, i, cc):
        landed(a, i, cc).wait_recv()
        forward(a, i, cc).start()

    send_out(X, 1, 1)
    over_peers(lambda i, cc: pass_on(COUNT, i, cc))
    for copy in load_rows[pieces:]:
        copy.wait()
    pick(G, me)
    plane(G, 0, 1 - c).start()
    keep_own(G).start()
    send_out(G, 2, 2)
    send_out(G, 1, 2, sending=False)

    def await_count(i, carry):
        for cc in range(2):
            forwarded(COUNT, i, cc).wait_recv()
        return carry

    lax.fori_loop(0, experts, await_count, 0)

    def table(r, start):
        load = packed[count_tile(r)][0:8, :].astype(F32)[0:1, :].astype(jnp.int32)
        starts[pl.ds(r, 1)] = start
        loads[pl.ds(r, 1)] = load
        return start + load

    lax.fori_loop(0, blocks, table, jnp.zeros((1, 128), jnp.int32))

    def packed_place(low, n):
        slot = lax.broadcasted_iota(jnp.int32, (n, capp, 128), 1)
        where = jnp.where(slot < loads[pl.ds(low, n)][:, None, :], slot + starts[pl.ds(low, n)][:, None, :], -1)
        return where.reshape(n * capp, 128)

    def pass_some(a, odd, low, high):
        def step(j, carry):
            i = 2 * j + odd
            for cc in range(2):

                @pl.when(jnp.logical_or(i > 0, cc != c))
                def _():
                    pass_on(a, i, cc)

            return carry

        lax.fori_loop(low, high, step, 0)

    windows = [row_window(k, blocks, cap, rows) for k in range(chunks)]

    def fetch_copy(a, k):
        low, high = windows[k]
        return pltpu.make_async_copy(land.at[a, pl.ds(low, high - low)], window.at[pl.ds(0, high - low)], local_sem.at[2])

    def fetch(a, k):
        before = -(-windows[k - 1][1] // 4) if k else 0

        def body(i, carry):
            for cc in range(2):
                forwarded(a, i, cc).wait_recv()
            return carry

        lax.fori_loop(before, -(-windows[k][1] // 4), body, 0)
        fetch_copy(a, k).start()

    def half_core(a, k, part):
        ref = (xbuf, gbuf)[a].at[lax.rem(k, 3), :, pl.ds(pl.multiple_of(part * half, half), half)]
        return remote(ref, ref, (half_sem.at[a, 0, k], half_sem.at[a, 1, k]), (me, over_c))

    def pack(a, k):
        low, high = windows[k]
        where = packed_place(low, high - low)
        number = lax.broadcasted_iota(jnp.int32, where.shape, 1) + k * CHUNK
        hot = jnp.concatenate([jnp.where(where == number + 128 * t, 1.0, 0.0).astype(BF16) for t in range(CHUNK // 128)], axis=1)
        fetch_copy(a, k).wait()
        block = dot_tn(hot, window[: high - low].reshape((high - low) * capp, half))
        (xbuf, gbuf)[a][k % 3, :, own_cols] = block.astype(BF16)
        half_core(a, k, c).start()

    STEP = 32

    def over_rows(count, body):
        def step(i, carry):
            body(pl.multiple_of(i * STEP, STEP))
            return carry

        lax.fori_loop(0, count // STEP, step, 0, unroll=4)

    def row_stats(v):
        mean = jnp.mean(v, axis=-1, keepdims=True)
        v = v - mean
        scale = lax.rsqrt(jnp.mean(v * v, axis=-1, keepdims=True) + EPS)
        return v * scale, scale

    def tiles(n):
        return [slice(t * 256, (t + 1) * 256) for t in range(n // 256)]

    def first(layer, normed, slot):
        for f in tiles(hidden):
            a = dot(normed(), wbuf[layer, 0, :, f]) + b_in[layer : layer + 1, f]
            sq = a * a
            t = jnp.tanh(a * (C1 + (C1 * C2) * sq))
            up = 0.5 + 0.5 * t
            ubuf[slot, 1, :, f] = (a * up).astype(BF16)
            ubuf[slot, 0, :, f] = (up + (0.5 * a) * (1.0 - t * t) * (C1 + (3.0 * C1 * C2) * sq)).astype(BF16)

    def second(layer, slot):
        for d in tiles(width):
            pscr[:, d] = dot(ubuf[slot, 1], wbuf[layer, 1, :, d])

    def back(layer, grad, slot, into):
        for f in tiles(hidden):
            da = (dot_nt(grad(), wbuf[layer, 1, f, :]) * ubuf[slot, 0, :, f].astype(F32)).astype(BF16)
            into[:, f] = da
            btally[layer, :, f] += fold(da.astype(F32))
        for d in tiles(width):
            pscr[:, d] = dot_nt(into[...], wbuf[layer, 0, d, :])

    def weight_grads(normed, grad, active, before):
        for f in tiles(hidden):
            acc_out[f, :] += dot_tn(active(f), grad())
        for d in tiles(width):
            acc_in[d, :] += dot_tn(normed(d), before())

    def split_rows(k, ring):
        own[ring] = pscr[own_rows]
        csend[ring] = pscr[other_rows].astype(BF16)

    def split_cols(ring):
        mown[...] = pscr[:, own_cols]
        msend[ring] = pscr[:, other_cols].astype(BF16)

    def fold(value):
        return jnp.sum(value.reshape(value.shape[0] // 8, 8, value.shape[1]), axis=0)

    def add_row(row, value):
        tally[row] += fold(value)

    GAIN0, GAIN1, SHIFT0, SHIFT1, BOUT0, BOUT1, CENT = range(7)

    def stage_a(k):
        ring, slot = lax.rem(k, 2), lax.rem(k, 3)
        half_core(X, k, 1 - c).wait_recv()
        save_x(k).start()

        def body(r):
            v = xbuf[slot, pl.ds(r, STEP)].astype(F32)
            share = jax.nn.sigmoid(jnp.sum(v * center[...], axis=-1, keepdims=True))
            stat[k, pl.ds(r, STEP), 0:1] = share
            unit, _ = row_stats(v)
            ubuf[ring, 2, pl.ds(r, STEP)] = (unit * gains[0:1] + shifts[0:1]).astype(BF16)


        @pl.when(k >= 2)
        def _():
            save_u(k - 2).wait()
            p_core(k - 2).wait_send()

        over_rows(CHUNK, body)
        first(0, lambda: ubuf[ring, 2], ring)
        save_u(k).start()
        second(0, ring)
        split_rows(k, ring)
        save_x(k).wait()
        half_core(X, k, c).wait_send()
        p_core(k).start()

    def stage_sum(k, core, over, which):
        core(k).wait_recv()
        ysend[which, k] = (own[lax.rem(k, 2)] + crecv[lax.rem(k, 4)].astype(F32)).astype(BF16)
        over(k).start()

    def loop1(k, carry):
        for i in range(1, chunks):

            @pl.when(k == i - 1)
            def _():
                pack(X, i)

        @pl.when(k < chunks)
        def _():
            stage_a(k)

        @pl.when(k == 0)
        def _():
            pass_some(X, 1, early, middle)

        @pl.when(k == 1)
        def _():
            pass_some(X, 1, middle, pairs)
            send_out(G, 1, 2, picking=False)

        for i in range(3, chunks):

            @pl.when(k == i)
            def _():
                pass_some(G, 1, (i - 3) * pairs // (chunks - 3), (i - 2) * pairs // (chunks - 3))

        for i in range(2, chunks):

            @pl.when(k == i - 2)
            def _():
                fetch(X, i)

        @pl.when(k >= 1)
        def _():
            stage_sum(k - 1, p_core, p_y, 0)

        return carry

    for copy in load_w(0):
        copy.wait()
    keep_own(X).wait()
    keep_own(G).wait()
    pairs = experts // 2
    early = -(-windows[1][1] // 8)
    middle = (early + pairs) // 2
    pass_some(X, 0, 0, pairs)
    pass_some(X, 1, 0, early // 2)
    forward_own(G).start()
    pass_some(G, 0, 0, pairs // 2)
    pass_some(X, 1, early // 2, early)
    fetch(X, 0)
    pass_some(G, 0, pairs // 2, pairs)
    pack(X, 0)
    fetch(X, 1)
    lax.fori_loop(0, chunks + 1, loop1, 0)
    for k in (chunks - 2, chunks - 1):
        save_u(k).wait()
        p_core(k).wait_send()
    load_x(0).start()
    fetch(G, 0)
    pack(G, 0)
    over_peers(lambda i, cc: plane(X, i, cc).wait_send())
    over_peers(lambda i, cc: plane(G, i, cc).wait_send())
    over_peers(lambda i, cc: forward(COUNT, i, cc).wait_send())
    for a in range(3):
        forward_own(a).wait_send()
    for copy in load_w(1):
        copy.wait()

    def stage_c(k):
        ring, slot = lax.rem(k, 2), lax.rem(k, 3)
        p_y(k).wait_recv()
        half_core(G, k, 1 - c).wait_recv()

        def body(r):
            here = pl.ds(r, STEP)
            there = pl.ds(pl.multiple_of(c * side + r, STEP), STEP)
            x = xbuf[slot, there].astype(F32)
            g = gbuf[slot, there].astype(F32)
            share = stat[k, there, 0:1]
            state = x + (ysend[0, k, here].astype(F32) + yrecv[0, k, here].astype(F32)) + b_out[0:1]
            unit, scale = row_stats(state)
            unit1[k, here] = unit.astype(BF16)
            stat[k, there, 2:3] = scale
            nbuf[k, c, here] = (unit * gains[1:2] + shifts[1:2]).astype(BF16)
            diff = state + b_out[1:2] - x
            base[ring, here] = 0.5 * (share * diff + x)
            pull = jnp.sum(g * diff, axis=-1, keepdims=True)
            stat[k, there, 1:2] = 0.5 * share * (1.0 - share) * pull

        over_rows(side, body)
        n_core(k, c).start()
        stat[k, other_rows, 1:2] = jnp.zeros((side, 1), F32)

    def stage_d(k):
        ring, slot = lax.rem(k, 2), lax.rem(k, 3)
        n_core(k, 1 - c).wait_recv()
        save_g(k).start()
        normed = lambda: nbuf[k].reshape(CHUNK, width)
        first(1, normed, 0)
        second(1, 0)

        def body(r, based):
            at = (c if based else 1 - c) * side + r
            there = pl.ds(pl.multiple_of(at, STEP), STEP)
            g = gbuf[slot, there].astype(F32)
            share = stat[k, there, 0:1]
            p = pscr[there]
            pull = jnp.sum(g * p, axis=-1, keepdims=True)
            stat[k, there, 1:2] = stat[k, there, 1:2] + share * (1.0 - share) * pull
            out = share * p
            if based:
                out = out + base[ring, pl.ds(r, STEP)]
            pscr[there] = out
            grad = share * g
            nscr[there] = grad.astype(BF16)
            add_row(BOUT1, 0.25 * grad)

        over_rows(side, functools.partial(body, based=True))
        over_rows(side, functools.partial(body, based=False))

        @pl.when(k >= 2)
        def _():
            m_core(k - 2).wait_send()
            d_core(k - 2).wait_send()

        split_cols(ring)
        m_core(k).start()
        back(1, lambda: nscr[...], 0, ascr)
        split_rows(k, ring)
        save_g(k).wait()
        half_core(G, k, c).wait_send()
        d_core(k).start()
        weight_grads(lambda d: nbuf[k, :, :, d].reshape(CHUNK, 256), lambda: nscr[...], lambda f: ubuf[0, 1, :, f], lambda: ascr[...])

    def stage_pack(k, core):
        core(k).wait_recv()
        packed[k] = (mown[...] + mrecv[lax.rem(k, 4)].astype(F32)).astype(BF16)

    def group_copy(a, g):
        part = pl.ds(g * span, span)
        return pltpu.make_async_remote_copy(
            src_ref=esend.at[part],
            dst_ref=erecv.at[a, part],
            send_sem=group_sem.at[a, 0, g],
            recv_sem=group_sem.at[a, 1, g],
            device_id=(me, over_y),
            device_id_type=MESH,
        )

    def plane_copy(a, d, cc):
        target = partner(d)
        return pltpu.make_async_remote_copy(
            src_ref=eown.at[d, cc],
            dst_ref=back_rows.at[a, c, me],
            send_sem=plane_sem.at[a, 0, d, cc],
            recv_sem=plane_sem.at[a, 1, d, c],
            device_id=(target, 2 * y + cc),
            device_id_type=MESH,
        )

    def plane_landed(a, d, cc):
        source = partner(d)
        ref = back_rows.at[a, cc, source]
        return pltpu.make_async_remote_copy(
            src_ref=ref,
            dst_ref=ref,
            send_sem=plane_sem.at[a, 0, d, cc],
            recv_sem=plane_sem.at[a, 1, d, cc],
            device_id=(me, over_y),
            device_id_type=MESH,
        )

    def group_rows(g):
        low = max(0, rows - cap * blocks + cap * 4 * g * span) // CHUNK
        high = min(chunks, -(-(cap * 4 * (g + 1) * span) // CHUNK))
        return low, high

    def expand(g, a):
        low, high = group_rows(g)
        if a:
            group_copy(0, g).wait_send()
        number = lax.broadcasted_iota(jnp.int32, (2 * capp, 128), 1) + low * CHUNK

        def part(i, yy, into):
            where = packed_place(4 * (g * span + i) + 2 * yy, 2)
            hot = jnp.concatenate(
                [jnp.where(where == number + 128 * t, 1.0, 0.0).astype(BF16) for t in range((high - low) * CHUNK // 128)], axis=1
            )
            block = dot(hot, packed[low:high].reshape((high - low) * CHUNK, half))
            into[g * span + i] = block.astype(BF16).reshape(2, capp, half)

        def far(i, carry):
            part(i, 1 - y, esend)
            return carry

        def near(i, carry):
            if a:
                finish(0, g * span + i)
            part(i, y, eown)
            return carry

        lax.fori_loop(0, span, far, 0)
        group_copy(a, g).start()
        lax.fori_loop(0, span, near, 0)

    def self_copy(a):
        return pltpu.make_async_copy(eown.at[0, c], back_rows.at[a, c, me], local_sem.at[1])

    def finish(a, d):
        @pl.when(d > 0)
        def _():
            plane_copy(a, d, 0).wait_send()
            plane_copy(a, d, 1).wait_send()

        @pl.when(d == 0)
        def _():
            plane_copy(a, 0, 1 - c).wait_send()
            self_copy(a).wait()

    def give_back(a, g):
        group_copy(a, g).wait_recv()

        def one(i, carry):
            d = g * span + i
            eown[d] = (eown[d].astype(F32) + erecv[a, d].astype(F32)).astype(BF16)

            @pl.when(d > 0)
            def _():
                plane_copy(a, d, 0).start()
                plane_copy(a, d, 1).start()

            @pl.when(d == 0)
            def _():
                plane_copy(a, 0, 1 - c).start()
                self_copy(a).start()

            return carry

        lax.fori_loop(0, span, one, 0)

    ready = [group_rows(g)[1] for g in range(groups)]
    late = sorted((g for g in range(groups) if ready[g] >= chunks), key=lambda g: (1 - g % 2, g))
    order = [g for g in range(groups) if g not in late] + late

    def loop2(k, carry):
        @pl.when(k < chunks)
        def _():
            load_x(k).wait()

        @pl.when(k + 1 < chunks)
        def _():
            load_x(k + 1).start()

        @pl.when(k >= 2)
        def _():
            stage_sum(k - 2, d_core, d_y, 1)

        for i in range(1, chunks):

            @pl.when(k == i - 1)
            def _():
                fetch(G, i)

        @pl.when(k < chunks)
        def _():
            stage_c(k)

        for i in range(1, chunks):

            @pl.when(k == i - 1)
            def _():
                pack(G, i)

        @pl.when(k >= 2)
        def _():
            stage_pack(k - 2, m_core)

        for g in range(groups):
            if ready[g] < chunks:

                @pl.when(k - 1 == ready[g])
                def _():
                    expand(g, 0)

        @pl.when(jnp.logical_and(k >= 1, k <= chunks))
        def _():
            stage_d(k - 1)

        return carry

    lax.fori_loop(0, chunks + 2, loop2, 0)
    for k in (chunks - 2, chunks - 1):
        m_core(k).wait_send()
        d_core(k).wait_send()

    def save_grads(layer):
        return pltpu.make_async_copy(wbuf.at[layer], gw.at[layer], w_sem.at[layer, 0])

    def round_grads(layer, wipe):
        def body(i, carry):
            rng = pl.ds(pl.multiple_of(i * 32, 32), 32)
            wbuf[layer, 0, rng] = acc_in[rng].astype(BF16)
            wbuf[layer, 1, rng] = acc_out[rng].astype(BF16)
            if wipe:
                acc_in[rng] = jnp.zeros((32, hidden), F32)
                acc_out[rng] = jnp.zeros((32, width), F32)
            return carry

        lax.fori_loop(0, width // 32, body, 0)

    round_grads(1, True)
    save_grads(1).start()
    load_x(0).start()
    load_g(0).start()
    load_u(0).start()
    for g in late:
        expand(g, 0)
    save_grads(1).wait()

    def stage_g(k):
        ring, slot = lax.rem(k, 2), lax.rem(k, 3)
        d_y(k).wait_recv()
        n_core(k, c).wait_send()

        def body(r):
            here = pl.ds(r, STEP)
            there = pl.ds(pl.multiple_of(c * side + r, STEP), STEP)
            g = gbuf[slot, there].astype(F32)
            share = stat[k, there, 0:1]
            dn = ysend[1, k, here].astype(F32) + yrecv[1, k, here].astype(F32)
            unit = unit1[k, here].astype(F32)
            w = dn * gains[1:2]
            add_row(GAIN1, 0.5 * dn * unit)
            add_row(SHIFT1, 0.5 * dn)
            grad = share * g + stat[k, there, 2:3] * (
                w - jnp.mean(w, axis=-1, keepdims=True) - unit * jnp.mean(w * unit, axis=-1, keepdims=True)
            )
            nbuf[k, c, here] = grad.astype(BF16)
            add_row(BOUT0, 0.5 * grad)
            base[ring, here] = 0.5 * (grad + (1.0 - share) * g)

        over_rows(side, body)
        dp_core(k, c).start()

    def before_at(k):
        per = chunks // 2
        return wbuf.at[1, k // per, pl.ds(pl.multiple_of(lax.rem(k, per) * CHUNK, CHUNK), CHUNK)]

    def stage_h(k):
        ring, slot = lax.rem(k, 2), lax.rem(k, 3)
        dp_core(k, 1 - c).wait_recv()
        back(0, lambda: nbuf[k].reshape(CHUNK, width), ring, before_at(k))

        def body(r, based):
            at = (c if based else 1 - c) * side + r
            there = pl.ds(pl.multiple_of(at, STEP), STEP)
            x = xbuf[slot, there].astype(F32)
            pull = stat[k, there, 1:2]
            unit, scale = row_stats(x)
            dn = pscr[there]
            w = dn * gains[0:1]
            add_row(GAIN0, dn * unit)
            add_row(SHIFT0, dn)
            add_row(CENT, pull * x)
            out = pull * center[...] + scale * (
                w - jnp.mean(w, axis=-1, keepdims=True) - unit * jnp.mean(w * unit, axis=-1, keepdims=True)
            )
            if based:
                out = out + base[ring, pl.ds(r, STEP)]
            pscr[there] = out

        over_rows(side, functools.partial(body, based=True))
        over_rows(side, functools.partial(body, based=False))

        @pl.when(k >= 2)
        def _():
            z_core(k - 2).wait_send()

        split_cols(ring)
        z_core(k).start()

    def stage_w(k, carry):
        load_un(k).wait()

        @pl.when(k + 1 < chunks)
        def _():
            load_un(k + 1).start()

        slot = lax.rem(k, 2)
        weight_grads(
            lambda d: ubuf[slot, 2, :, d],
            lambda: nbuf[k].reshape(CHUNK, width),
            lambda f: ubuf[slot, 1, :, f],
            lambda: before_at(k)[...],
        )
        return carry

    def loop3(k, carry):
        @pl.when(k < chunks)
        def _():
            load_x(k).wait()
            load_g(k).wait()

        @pl.when(k + 1 < chunks)
        def _():
            load_x(k + 1).start()
            load_g(k + 1).start()

        @pl.when(k >= 2)
        def _():
            stage_pack(k - 2, z_core)

        @pl.when(k < chunks)
        def _():
            stage_g(k)

        @pl.when(k >= 1)
        def _():
            load_u(k - 1).wait()

        @pl.when(jnp.logical_and(k >= 1, k < chunks))
        def _():
            load_u(k).start()

        @pl.when(k >= 1)
        def _():
            stage_h(k - 1)

        for n, g in enumerate(order):

            @pl.when(k == 1 + n * chunks // groups)
            def _():
                give_back(0, g)

        for g in range(groups):
            if ready[g] < chunks:

                @pl.when(k - 1 == ready[g])
                def _():
                    expand(g, 1)

        return carry

    lax.fori_loop(0, chunks + 1, loop3, 0)
    stage_pack(chunks - 1, z_core)
    for g in late:
        expand(g, 1)
    load_un(0).start()

    for row in range(8):
        mine[row : row + 1] = jnp.sum(tally[row], axis=0, keepdims=True)
    for layer in range(SUBLAYERS):
        gb_in[layer : layer + 1] = jnp.sum(btally[layer], axis=0, keepdims=True)
    tallies[place] = mine[...]

    def tally_copy(i, to):
        return pltpu.make_async_remote_copy(
            src_ref=mine,
            dst_ref=tallies.at[place],
            send_sem=sum_sem.at[0, i],
            recv_sem=sum_sem.at[1, i],
            device_id=(me, to),
            device_id_type=MESH,
        )

    def tally_landed(i, frm):
        ref = tallies.at[frm]
        return pltpu.make_async_remote_copy(
            src_ref=ref, dst_ref=ref, send_sem=sum_sem.at[0, i], recv_sem=sum_sem.at[1, i], device_id=(me, frm), device_id_type=MESH
        )

    others = (over_c, over_y, over_both)
    for i, to in enumerate(others):
        tally_copy(i, to).start()
    for g in order[: groups - len(late)]:
        give_back(1, g)
    lax.fori_loop(0, chunks // 2, stage_w, 0)
    give_back(1, late[0])
    lax.fori_loop(chunks // 2, chunks, stage_w, 0)
    give_back(1, late[1])
    round_grads(0, False)
    save_grads(0).start()
    for g in late[2:]:
        give_back(1, g)

    def gather_back(a, result):
        def wait(d, carry):
            for cc in range(2):

                @pl.when(jnp.logical_or(d > 0, cc != c))
                def _():
                    plane_landed(a, d, cc).wait_recv()

            return carry

        lax.fori_loop(0, experts, wait, 0)
        if a:
            self_copy(1).wait()
        lane = lax.broadcasted_iota(jnp.int32, (experts * capp, 128), 1)
        where = slots[...].reshape(experts * capp, 128)
        for j in range(2):
            copy = pltpu.make_async_copy(back_rows.at[a, j], window.at[pl.ds(0, experts)], local_sem.at[0])
            copy.start()
            copy.wait()
            for i, hold in enumerate((nscr, ascr)):
                hot = jnp.concatenate(
                    [jnp.where(where == lane + (i * CHUNK + 128 * t), 1.0, 0.0).astype(BF16) for t in range(CHUNK // 128)], axis=1
                )
                block = window[:experts]
                hold[:, j * half : (j + 1) * half] = dot_tn(hot, block.reshape(experts * capp, half)).astype(BF16)
        for i, hold in enumerate((nscr, ascr)):
            pltpu.make_async_copy(hold, result.at[pl.ds(i * CHUNK, CHUNK)], local_sem.at[2 + i]).start()

    def gathered(result):
        for i, hold in enumerate((nscr, ascr)):
            pltpu.make_async_copy(hold, result.at[pl.ds(i * CHUNK, CHUNK)], local_sem.at[2 + i]).wait()

    gather_back(0, mixed)
    for i, frm in enumerate(others):
        tally_landed(i, frm).wait_recv()
        tally_copy(i, frm).wait_send()
    sums[...] = (tallies[0] + tallies[1]) + (tallies[2] + tallies[3])
    gathered(mixed)
    gather_back(1, gtok)
    for g in range(groups):
        group_copy(1, g).wait_send()

    def last(d, carry):
        @pl.when(d > 0)
        def _():
            plane_copy(1, d, 0).wait_send()
            plane_copy(1, d, 1).wait_send()

        @pl.when(d == 0)
        def _():
            plane_copy(1, 0, 1 - c).wait_send()

        return carry

    lax.fori_loop(0, experts, last, 0)

    over_peers(lambda i, cc: plane(COUNT, i, cc).wait_send())
    for a in (X, G):
        over_peers(lambda i, cc: forward(a, i, cc).wait_send())

    def last_chunk(k, carry):
        p_y(k).wait_send()
        d_y(k).wait_send()
        dp_core(k, c).wait_send()
        return carry

    lax.fori_loop(0, chunks, last_chunk, 0)
    for k in (chunks - 2, chunks - 1):
        z_core(k).wait_send()
    save_grads(0).wait()
    gathered(gtok)


def finish_kernel(mixed, gtok, gw, gb_in, sums, mixed_out, gtok_out, gw_in, gw_out, gb_in_out, gain, shift, b_out, center):
    mixed_out[...] = mixed[...]
    gtok_out[...] = gtok[...].astype(F32)
    gw_in[...] = gw[:, 0].astype(F32)
    gw_out[...] = gw[:, 1].astype(F32)
    gb_in_out[...] = gb_in[...]
    gain[...] = sums[0:2]
    shift[...] = sums[2:4]
    b_out[...] = sums[4:6]
    center[...] = sums[6:7]


def finish(mixed, gtok, gw, gb_in, sums):
    toks, width = mixed.shape
    steps = 8
    rows = pl.BlockSpec((toks // steps, width), lambda i: (i, 0))
    weight = pl.BlockSpec((SUBLAYERS, width // steps, width), lambda i: (0, i, 0))

    def whole(n):
        return pl.BlockSpec((n, width), lambda i: (0, 0))

    def shape(*dims):
        return jax.ShapeDtypeStruct(dims, F32)

    return pl.pallas_call(
        finish_kernel,
        grid=(steps,),
        out_shape=(
            jax.ShapeDtypeStruct((toks, width), BF16),
            shape(toks, width),
            shape(SUBLAYERS, width, width),
            shape(SUBLAYERS, width, width),
            shape(SUBLAYERS, width),
            shape(SUBLAYERS, width),
            shape(SUBLAYERS, width),
            shape(SUBLAYERS, width),
            shape(1, width),
        ),
        in_specs=[
            rows,
            rows,
            pl.BlockSpec((SUBLAYERS, 2, width // steps, width), lambda i: (0, 0, i, 0)),
            whole(SUBLAYERS),
            whole(8),
        ],
        out_specs=(rows, rows, weight, weight, whole(2), whole(2), whole(2), whole(2), whole(1)),
        compiler_params=pltpu.CompilerParams(vmem_limit_bytes=32 * 2**20),
        name="finish",
    )(mixed, gtok, gw, gb_in, sums)


def layers(cap, slots, tok, cot, w_in, w_out, b_in, b_out, gains, shifts, center):
    experts, capp = slots.shape[:2]
    blocks = 4 * experts
    toks, width = tok.shape
    rows = 4 * toks
    hidden = b_in.shape[1]
    half, side, chunks = width // 2, CHUNK // 2, rows // CHUNK
    span = experts // GROUPS
    windows = [row_window(k, blocks, cap, rows) for k in range(chunks)]
    reach = max(high - low for low, high in windows)
    vmem = pl.BlockSpec(memory_space=pltpu.VMEM)
    hbm = pl.BlockSpec(memory_space=pl.ANY)
    dma = pltpu.SemaphoreType.DMA
    return pl.pallas_call(
        functools.partial(layers_kernel, experts, cap),
        out_shape=(
            jax.ShapeDtypeStruct((toks, width), BF16),
            jax.ShapeDtypeStruct((toks, width), BF16),
            jax.ShapeDtypeStruct((SUBLAYERS, 2, width, width), BF16),
            jax.ShapeDtypeStruct((SUBLAYERS, hidden), F32),
            jax.ShapeDtypeStruct((8, width), F32),
            jax.ShapeDtypeStruct((chunks, 3, CHUNK, hidden), BF16),
            jax.ShapeDtypeStruct((2, 2, experts, capp, half), BF16),
            jax.ShapeDtypeStruct((2, blocks, capp, half), BF16),
            jax.ShapeDtypeStruct((rows, width), BF16),
            jax.ShapeDtypeStruct((rows, width), BF16),
        ),
        in_specs=[vmem, hbm, hbm, hbm, hbm, vmem, vmem, vmem, vmem, vmem],
        out_specs=(hbm, hbm, hbm, vmem, vmem, hbm, hbm, hbm, hbm, hbm),
        scratch_shapes=[
            pltpu.VMEM((SUBLAYERS, 2, width, width), BF16),
            pltpu.VMEM((width, hidden), F32),
            pltpu.VMEM((hidden, width), F32),
            pltpu.VMEM((3, CHUNK, width), BF16),
            pltpu.VMEM((3, CHUNK, width), BF16),
            pltpu.VMEM((reach, capp, half), BF16),
            pltpu.VMEM((blocks, 128), jnp.int32),
            pltpu.VMEM((blocks, 128), jnp.int32),
            pltpu.VMEM((experts, 16, 128), BF16),
            pltpu.VMEM((2, 3, CHUNK, hidden), BF16),
            pltpu.VMEM((chunks, 2, side, width), BF16),
            pltpu.VMEM((CHUNK, width), BF16),
            pltpu.VMEM((CHUNK, hidden), BF16),
            pltpu.VMEM((CHUNK, width), F32),
            pltpu.VMEM((2, side, width), F32),
            pltpu.VMEM((2, side, width), BF16),
            pltpu.VMEM((4, side, width), BF16),
            pltpu.VMEM((2, chunks, side, width), BF16),
            pltpu.VMEM((2, chunks, side, width), BF16),
            pltpu.VMEM((chunks, side, width), BF16),
            pltpu.VMEM((2, side, width), F32),
            pltpu.VMEM((chunks, CHUNK, 128), F32),
            pltpu.VMEM((CHUNK, half), F32),
            pltpu.VMEM((2, CHUNK, half), BF16),
            pltpu.VMEM((4, CHUNK, half), BF16),
            pltpu.VMEM((chunks, CHUNK, half), BF16),
            pltpu.VMEM((experts, 2, capp, half), BF16),
            pltpu.VMEM((experts, 2, capp, half), BF16),
            pltpu.VMEM((2, experts, 2, capp, half), BF16),
            pltpu.VMEM((8, 8, width), F32),
            pltpu.VMEM((SUBLAYERS, 8, hidden), F32),
            pltpu.VMEM((8, width), F32),
            pltpu.VMEM((4, 8, width), F32),
            dma((8, 2, chunks)),
            dma((2, 2, GROUPS)),
            dma((2, 2, experts, 2)),
            dma((2, 3)),
            dma((SUBLAYERS, 2)),
            dma((3,)),
            dma((3,)),
            dma((2, 2)),
            dma((4,)),
            dma((3, 4, experts, 2)),
            dma((2, 2, chunks)),
        ],
        compiler_params=pltpu.CompilerParams(collective_id=0, has_side_effects=True, vmem_limit_bytes=62 * 2**20),
        name="layers",
    )(slots, tok, cot, w_in, w_out, b_in, b_out, gains, shifts, center)


def on_device(experts, places, tokens, dispatch_rows, w_in, w_out, b_in, b_out, ln_gain, ln_bias, centroid, cotangent):
    slots = dispatch_rows[0]
    toks = tokens.shape[0]
    cap = slots.shape[1]
    capp = -(-cap // 16) * 16
    padded = jnp.pad(slots, ((0, 0), (0, capp - cap)), constant_values=toks)
    spread = jnp.broadcast_to(padded[:, :, None], (experts, capp, 128))
    parts = layers(cap, spread, tokens, cotangent, w_in[0], w_out[0], b_in[0], b_out[0], ln_gain[0], ln_bias[0], centroid)
    mixed, gtok, gw_in, gw_out, gb_in, gain, shift, bias, center = finish(*parts[:5])
    return mixed, gtok, gw_in[None], gw_out[None], gb_in[None], bias[None], gain[None], shift[None], center


def solution(mesh):
    rows = P(("expert", "hidden"), None)
    return jax.shard_map(
        functools.partial(on_device, mesh.shape["expert"], mesh.shape["hidden"]),
        mesh=mesh,
        in_specs=(
            rows,
            P(("expert", "hidden"), None, None),
            P("expert", None, None, "hidden"),
            P("expert", None, "hidden", None),
            P("expert", None, "hidden"),
            P("expert", None, None),
            P("expert", None, None),
            P("expert", None, None),
            P("expert", None),
            rows,
        ),
        out_specs=(
            rows,
            rows,
            P("expert", None, None, "hidden"),
            P("expert", None, "hidden", None),
            P("expert", None, "hidden"),
            P("expert", None, None),
            P("expert", None, None),
            P("expert", None, None),
            P("expert", None),
        ),
        check_vma=False,
    )
```

```python
import functools

import jax
import jax.numpy as jnp
from jax import lax
from jax.experimental import pallas as pl
from jax.experimental.pallas import tpu as pltpu
from jax.sharding import PartitionSpec as P

MESH = pl.DeviceIdType.MESH
SUBLAYERS = 2
EPS = 1e-05
F32 = jnp.float32
BF16 = jnp.bfloat16
CHUNK = 256
GROUPS = 8
C1 = 0.7978845608028654
C2 = 0.044715


def dot(left, right):
    return jnp.dot(left, right, preferred_element_type=F32)


def dot_tn(left, right):
    return lax.dot_general(left, right, (((0,), (0,)), ((), ())), preferred_element_type=F32)


def dot_nt(left, right):
    return lax.dot_general(left, right, (((1,), (1,)), ((), ())), preferred_element_type=F32)


def row_window(chunk, blocks, cap, rows):
    low = (chunk * CHUNK) // cap
    high = min(blocks - 1, (chunk * CHUNK + CHUNK - 1 + cap * blocks - rows) // cap)
    return low, high + 1


def layers_kernel(
    experts,
    cap,
    slots, tok, cot, w_in, w_out, b_in, b_out, gains, shifts, center,
    mixed, gtok, gw, gb_in, sums, spill, back_rows, land, xc, gc,
    wbuf, acc_in, acc_out, xbuf, gbuf, window, starts, loads, tell, ubuf, nbuf, nscr, ascr, pscr, own, csend, crecv,
    ysend, yrecv, unit1, base, stat, mown, msend, mrecv, packed, esend, eown, erecv, tally, btally, mine, tallies,
    chunk_sem, group_sem, plane_sem, sum_sem, w_sem, x_sem, g_sem, u_sem, local_sem, in_sem, half_sem,
):
    me = lax.axis_index("expert")
    place = lax.axis_index("hidden")
    y = place // 2
    c = lax.rem(place, 2)
    over_y = lax.rem(place + 2, 4)
    over_c = place + 1 - 2 * c
    over_both = 3 - place
    rows, width = xc.shape
    chunks = rows // CHUNK
    hidden = b_in.shape[1]
    half = width // 2
    side = CHUNK // 2
    toks = mixed.shape[0]
    capp = slots.shape[1]
    blocks = 4 * experts
    groups = GROUPS
    span = experts // groups

    barrier = pltpu.get_barrier_semaphore()

    def greet(i, carry):
        e = lax.rem(me + i // 2, experts)
        cc = lax.rem(i, 2)

        @pl.when(jnp.logical_or(i // 2 > 0, cc != c))
        def _():
            pl.semaphore_signal(barrier, 1, device_id=(e, 2 * y + cc), device_id_type=MESH)

        return carry

    lax.fori_loop(0, 2 * experts, greet, 0)
    pl.semaphore_signal(barrier, 1, device_id=(me, over_y), device_id_type=MESH)
    pl.semaphore_signal(barrier, 1, device_id=(me, over_both), device_id_type=MESH)

    own_rows = pl.ds(pl.multiple_of(c * side, side), side)
    other_rows = pl.ds(pl.multiple_of((1 - c) * side, side), side)
    own_cols = pl.ds(pl.multiple_of(c * half, half), half)
    other_cols = pl.ds(pl.multiple_of((1 - c) * half, half), half)

    def send(src, dst, kind, k, to):
        return pltpu.make_async_remote_copy(
            src_ref=src,
            dst_ref=dst,
            send_sem=chunk_sem.at[kind, 0, k],
            recv_sem=chunk_sem.at[kind, 1, k],
            device_id=(me, to),
            device_id_type=MESH,
        )

    P_CORE, P_Y, N_CORE, M_CORE, D_CORE, D_Y, DP_CORE, Z_CORE = range(8)

    def p_core(k):
        return send(csend.at[lax.rem(k, 2)], crecv.at[lax.rem(k, 4)], P_CORE, k, over_c)

    def d_core(k):
        return send(csend.at[lax.rem(k, 2)], crecv.at[lax.rem(k, 4)], D_CORE, k, over_c)

    def p_y(k):
        return send(ysend.at[0, k], yrecv.at[0, k], P_Y, k, over_y)

    def d_y(k):
        return send(ysend.at[1, k], yrecv.at[1, k], D_Y, k, over_y)

    def n_core(k, part):
        return send(nbuf.at[k, part], nbuf.at[k, part], N_CORE, k, over_c)

    def dp_core(k, part):
        return send(nbuf.at[k, part], nbuf.at[k, part], DP_CORE, k, over_c)

    def m_core(k):
        return send(msend.at[lax.rem(k, 2)], mrecv.at[lax.rem(k, 4)], M_CORE, k, over_c)

    def z_core(k):
        return send(msend.at[lax.rem(k, 2)], mrecv.at[lax.rem(k, 4)], Z_CORE, k, over_c)

    def load_x(k):
        return pltpu.make_async_copy(xc.at[pl.ds(k * CHUNK, CHUNK)], xbuf.at[lax.rem(k, 3)], x_sem.at[lax.rem(k, 3)])

    def load_g(k):
        return pltpu.make_async_copy(gc.at[pl.ds(k * CHUNK, CHUNK)], gbuf.at[lax.rem(k, 3)], g_sem.at[lax.rem(k, 3)])

    def save_g(k):
        return pltpu.make_async_copy(gbuf.at[lax.rem(k, 3)], gc.at[pl.ds(k * CHUNK, CHUNK)], g_sem.at[lax.rem(k, 3)])

    def save_x(k):
        return pltpu.make_async_copy(xbuf.at[lax.rem(k, 3)], xc.at[pl.ds(k * CHUNK, CHUNK)], x_sem.at[lax.rem(k, 3)])

    def save_u(k):
        return pltpu.make_async_copy(ubuf.at[lax.rem(k, 2)], spill.at[k], u_sem.at[lax.rem(k, 2), 0])

    def load_u(k):
        return pltpu.make_async_copy(spill.at[k, 0], ubuf.at[lax.rem(k, 2), 0], u_sem.at[lax.rem(k, 2), 0])

    def load_un(k):
        return pltpu.make_async_copy(spill.at[k, pl.ds(1, 2)], ubuf.at[lax.rem(k, 2), pl.ds(1, 2)], u_sem.at[lax.rem(k, 2), 0])

    def load_w(layer):
        return (
            pltpu.make_async_copy(w_in.at[layer], wbuf.at[layer, 0], w_sem.at[layer, 0]),
            pltpu.make_async_copy(w_out.at[layer], wbuf.at[layer, 1], w_sem.at[layer, 1]),
        )

    for layer in range(SUBLAYERS):
        for copy in load_w(layer):
            copy.start()
    pieces = toks // CHUNK
    load_rows = [
        pltpu.make_async_copy(ref.at[pl.ds(i * CHUNK, CHUNK)], ubuf.at[a, i], u_sem.at[a, i])
        for a, ref in enumerate((tok, cot))
        for i in range(pieces)
    ]
    for copy in load_rows:
        copy.start()
    tally[...] = jnp.zeros_like(tally)
    btally[...] = jnp.zeros_like(btally)

    def clear(acc):
        def body(i, carry):
            acc[pl.ds(pl.multiple_of(i * 32, 32), 32)] = jnp.zeros((32, acc.shape[1]), F32)
            return carry

        lax.fori_loop(0, acc.shape[0] // 32, body, 0)

    clear(acc_in)
    clear(acc_out)
    bits = experts.bit_length() - 1

    def partner(i):
        return sum(lax.rem(me // 2**j + i // 2 ** (bits - 1 - j), 2) * 2**j for j in range(bits))


    X, G, COUNT = range(3)
    picked = (esend, eown)

    def rank(i, yy, cc):
        return i * 4 + yy * 2 + cc

    def count_tile(r):
        down, across = CHUNK // 16, half // 128
        return (
            r // (down * across),
            pl.ds(pl.multiple_of(lax.rem(r, down) * 16, 16), 16),
            pl.ds(pl.multiple_of(lax.rem(r // down, across) * 128, 128), 128),
        )

    def place_of(a, r):
        return packed.at[count_tile(r)] if a == COUNT else land.at[a, r]

    def remote(src, dst, sems, to):
        return pltpu.make_async_remote_copy(
            src_ref=src, dst_ref=dst, send_sem=sems[0], recv_sem=sems[1], device_id=to, device_id_type=MESH
        )

    def plane(a, i, cc):
        target = partner(i)
        src = tell.at[target] if a == COUNT else picked[a].at[target, cc]
        return remote(src, place_of(a, rank(i, y, c)), (in_sem.at[a, 0, i, cc], in_sem.at[a, 1, i, c]), (target, 2 * y + cc))

    def landed(a, i, cc):
        ref = place_of(a, rank(i, y, cc))
        return remote(ref, ref, (in_sem.at[a, 0, i, cc], in_sem.at[a, 1, i, cc]), (me, over_y))

    def forward(a, i, cc):
        ref = place_of(a, rank(i, y, cc))
        return remote(ref, ref, (in_sem.at[a, 2, i, cc], in_sem.at[a, 3, i, cc]), (me, over_y))

    def forward_own(a):
        src = tell.at[me] if a == COUNT else picked[a].at[me, c]
        return remote(src, place_of(a, rank(0, y, c)), (in_sem.at[a, 2, 0, c], in_sem.at[a, 3, 0, c]), (me, over_y))

    def forwarded(a, i, cc):
        ref = place_of(a, rank(i, 1 - y, cc))
        return remote(ref, ref, (in_sem.at[a, 2, i, cc], in_sem.at[a, 3, i, cc]), (me, over_y))

    def keep_own(a):
        return pltpu.make_async_copy(picked[a].at[me, c], land.at[a, rank(0, y, c)], local_sem.at[a])

    def over_peers(body, first=0):
        def step(i, carry):
            for cc in range(2):

                @pl.when(jnp.logical_or(i > 0, cc != c))
                def _():
                    body(i, cc)

            return carry

        lax.fori_loop(first, experts, step, 0)

    token = lax.broadcasted_iota(jnp.int32, (capp, 128), 1)

    def count(target):
        load = jnp.sum(jnp.where(slots[target] < toks, 1.0, 0.0), axis=0, keepdims=True)
        tell[target] = jnp.broadcast_to(load, (16, 128)).astype(BF16)

    def pick(a, target):
        where = slots[target]
        hot = jnp.concatenate([jnp.where(where == token + 128 * t, 1.0, 0.0).astype(BF16) for t in range(toks // 128)], axis=1)
        block = dot(hot, ubuf[a, :pieces].reshape(toks, width)).astype(BF16)
        picked[a][target, 0] = block[:, :half]
        picked[a][target, 1] = block[:, half:]

    def count_all(i, carry):
        count(i)
        return carry

    lax.fori_loop(0, experts, count_all, 0)
    packed[count_tile(rank(0, y, c))] = tell[me]
    for copy in load_rows[:pieces]:
        copy.wait()
    pick(X, me)
    pl.semaphore_wait(barrier, 2 * experts + 1)
    over_peers(lambda i, cc: plane(COUNT, i, cc).start())
    forward_own(COUNT).start()
    plane(X, 0, 1 - c).start()
    forward_own(X).start()
    keep_own(X).start()

    def send_out(a, first, step, picking=True, sending=True):
        def body(j, carry):
            i = first + j * step
            if picking:
                pick(a, partner(i))
            if sending:
                plane(a, i, 0).start()
                plane(a, i, 1).start()
            return carry

        lax.fori_loop(0, -(-(experts - first) // step), body, 0)

    def pass_on(a, i, cc):
        landed(a, i, cc).wait_recv()
        forward(a, i, cc).start()

    send_out(X, 1, 1)
    over_peers(lambda i, cc: pass_on(COUNT, i, cc))
    for copy in load_rows[pieces:]:
        copy.wait()
    pick(G, me)
    plane(G, 0, 1 - c).start()
    keep_own(G).start()
    send_out(G, 2, 2)
    send_out(G, 1, 2, sending=False)

    def await_count(i, carry):
        for cc in range(2):
            forwarded(COUNT, i, cc).wait_recv()
        return carry

    lax.fori_loop(0, experts, await_count, 0)

    def table(r, start):
        load = packed[count_tile(r)][0:8, :].astype(F32)[0:1, :].astype(jnp.int32)
        starts[pl.ds(r, 1)] = start
        loads[pl.ds(r, 1)] = load
        return start + load

    lax.fori_loop(0, blocks, table, jnp.zeros((1, 128), jnp.int32))

    def packed_place(low, n):
        slot = lax.broadcasted_iota(jnp.int32, (n, capp, 128), 1)
        where = jnp.where(slot < loads[pl.ds(low, n)][:, None, :], slot + starts[pl.ds(low, n)][:, None, :], -1)
        return where.reshape(n * capp, 128)

    def pass_some(a, odd, low, high):
        def step(j, carry):
            i = 2 * j + odd
            for cc in range(2):

                @pl.when(jnp.logical_or(i > 0, cc != c))
                def _():
                    pass_on(a, i, cc)

            return carry

        lax.fori_loop(low, high, step, 0)

    windows = [row_window(k, blocks, cap, rows) for k in range(chunks)]

    def fetch_copy(a, k):
        low, high = windows[k]
        return pltpu.make_async_copy(land.at[a, pl.ds(low, high - low)], window.at[pl.ds(0, high - low)], local_sem.at[2])

    def fetch(a, k):
        before = -(-windows[k - 1][1] // 4) if k else 0

        def body(i, carry):
            for cc in range(2):
                forwarded(a, i, cc).wait_recv()
            return carry

        lax.fori_loop(before, -(-windows[k][1] // 4), body, 0)
        fetch_copy(a, k).start()

    def half_core(a, k, part):
        ref = (xbuf, gbuf)[a].at[lax.rem(k, 3), :, pl.ds(pl.multiple_of(part * half, half), half)]
        return remote(ref, ref, (half_sem.at[a, 0, k], half_sem.at[a, 1, k]), (me, over_c))

    def pack(a, k):
        low, high = windows[k]
        where = packed_place(low, high - low)
        number = lax.broadcasted_iota(jnp.int32, where.shape, 1) + k * CHUNK
        hot = jnp.concatenate([jnp.where(where == number + 128 * t, 1.0, 0.0).astype(BF16) for t in range(CHUNK // 128)], axis=1)
        fetch_copy(a, k).wait()
        block = dot_tn(hot, window[: high - low].reshape((high - low) * capp, half))
        (xbuf, gbuf)[a][k % 3, :, own_cols] = block.astype(BF16)
        half_core(a, k, c).start()

    STEP = 32

    def over_rows(count, body):
        def step(i, carry):
            body(pl.multiple_of(i * STEP, STEP))
            return carry

        lax.fori_loop(0, count // STEP, step, 0, unroll=4)

    def row_stats(v):
        mean = jnp.mean(v, axis=-1, keepdims=True)
        v = v - mean
        scale = lax.rsqrt(jnp.mean(v * v, axis=-1, keepdims=True) + EPS)
        return v * scale, scale

    def tiles(n):
        return [slice(t * 256, (t + 1) * 256) for t in range(n // 256)]

    def first(layer, normed, slot):
        for f in tiles(hidden):
            a = dot(normed(), wbuf[layer, 0, :, f]) + b_in[layer : layer + 1, f]
            sq = a * a
            t = jnp.tanh(a * (C1 + (C1 * C2) * sq))
            up = 0.5 + 0.5 * t
            ubuf[slot, 1, :, f] = (a * up).astype(BF16)
            ubuf[slot, 0, :, f] = (up + (0.5 * a) * (1.0 - t * t) * (C1 + (3.0 * C1 * C2) * sq)).astype(BF16)

    def second(layer, slot):
        for d in tiles(width):
            pscr[:, d] = dot(ubuf[slot, 1], wbuf[layer, 1, :, d])

    def back(layer, grad, slot, into):
        for f in tiles(hidden):
            da = (dot_nt(grad(), wbuf[layer, 1, f, :]) * ubuf[slot, 0, :, f].astype(F32)).astype(BF16)
            into[:, f] = da
            btally[layer, :, f] += fold(da.astype(F32))
        for d in tiles(width):
            pscr[:, d] = dot_nt(into[...], wbuf[layer, 0, d, :])

    def weight_grads(normed, grad, active, before):
        for f in tiles(hidden):
            acc_out[f, :] += dot_tn(active(f), grad())
        for d in tiles(width):
            acc_in[d, :] += dot_tn(normed(d), before())

    def split_rows(k, ring):
        own[ring] = pscr[own_rows]
        csend[ring] = pscr[other_rows].astype(BF16)

    def split_cols(ring):
        mown[...] = pscr[:, own_cols]
        msend[ring] = pscr[:, other_cols].astype(BF16)

    def fold(value):
        return jnp.sum(value.reshape(value.shape[0] // 8, 8, value.shape[1]), axis=0)

    def add_row(row, value):
        tally[row] += fold(value)

    GAIN0, GAIN1, SHIFT0, SHIFT1, BOUT0, BOUT1, CENT = range(7)

    def stage_a(k):
        ring, slot = lax.rem(k, 2), lax.rem(k, 3)
        half_core(X, k, 1 - c).wait_recv()
        save_x(k).start()

        def body(r):
            v = xbuf[slot, pl.ds(r, STEP)].astype(F32)
            share = jax.nn.sigmoid(jnp.sum(v * center[...], axis=-1, keepdims=True))
            stat[k, pl.ds(r, STEP), 0:1] = share
            unit, _ = row_stats(v)
            ubuf[ring, 2, pl.ds(r, STEP)] = (unit * gains[0:1] + shifts[0:1]).astype(BF16)


        @pl.when(k >= 2)
        def _():
            save_u(k - 2).wait()
            p_core(k - 2).wait_send()

        over_rows(CHUNK, body)
        first(0, lambda: ubuf[ring, 2], ring)
        save_u(k).start()
        second(0, ring)
        split_rows(k, ring)
        save_x(k).wait()
        half_core(X, k, c).wait_send()
        p_core(k).start()

    def stage_sum(k, core, over, which):
        core(k).wait_recv()
        ysend[which, k] = (own[lax.rem(k, 2)] + crecv[lax.rem(k, 4)].astype(F32)).astype(BF16)
        over(k).start()

    def loop1(k, carry):
        for i in range(1, chunks):

            @pl.when(k == i - 1)
            def _():
                pack(X, i)

        @pl.when(k < chunks)
        def _():
            stage_a(k)

        @pl.when(k == 0)
        def _():
            pass_some(X, 1, early, middle)

        @pl.when(k == 1)
        def _():
            pass_some(X, 1, middle, pairs)
            send_out(G, 1, 2, picking=False)

        for i in range(3, chunks):

            @pl.when(k == i)
            def _():
                pass_some(G, 1, (i - 3) * pairs // (chunks - 3), (i - 2) * pairs // (chunks - 3))

        for i in range(2, chunks):

            @pl.when(k == i - 2)
            def _():
                fetch(X, i)

        @pl.when(k >= 1)
        def _():
            stage_sum(k - 1, p_core, p_y, 0)

        return carry

    for copy in load_w(0):
        copy.wait()
    keep_own(X).wait()
    keep_own(G).wait()
    pairs = experts // 2
    early = -(-windows[1][1] // 8)
    middle = (early + pairs) // 2
    pass_some(X, 0, 0, pairs)
    pass_some(X, 1, 0, early // 2)
    forward_own(G).start()
    pass_some(G, 0, 0, pairs // 2)
    pass_some(X, 1, early // 2, early)
    fetch(X, 0)
    pass_some(G, 0, pairs // 2, pairs)
    pack(X, 0)
    fetch(X, 1)
    lax.fori_loop(0, chunks + 1, loop1, 0)
    for k in (chunks - 2, chunks - 1):
        save_u(k).wait()
        p_core(k).wait_send()
    load_x(0).start()
    fetch(G, 0)
    pack(G, 0)
    over_peers(lambda i, cc: plane(X, i, cc).wait_send())
    over_peers(lambda i, cc: plane(G, i, cc).wait_send())
    over_peers(lambda i, cc: forward(COUNT, i, cc).wait_send())
    for a in range(3):
        forward_own(a).wait_send()
    for copy in load_w(1):
        copy.wait()

    def stage_c(k):
        ring, slot = lax.rem(k, 2), lax.rem(k, 3)
        p_y(k).wait_recv()
        half_core(G, k, 1 - c).wait_recv()

        def body(r):
            here = pl.ds(r, STEP)
            there = pl.ds(pl.multiple_of(c * side + r, STEP), STEP)
            x = xbuf[slot, there].astype(F32)
            g = gbuf[slot, there].astype(F32)
            share = stat[k, there, 0:1]
            state = x + (ysend[0, k, here].astype(F32) + yrecv[0, k, here].astype(F32)) + b_out[0:1]
            unit, scale = row_stats(state)
            unit1[k, here] = unit.astype(BF16)
            stat[k, there, 2:3] = scale
            nbuf[k, c, here] = (unit * gains[1:2] + shifts[1:2]).astype(BF16)
            diff = state + b_out[1:2] - x
            base[ring, here] = 0.5 * (share * diff + x)
            pull = jnp.sum(g * diff, axis=-1, keepdims=True)
            stat[k, there, 1:2] = 0.5 * share * (1.0 - share) * pull

        over_rows(side, body)
        n_core(k, c).start()
        stat[k, other_rows, 1:2] = jnp.zeros((side, 1), F32)

    def stage_d(k):
        ring, slot = lax.rem(k, 2), lax.rem(k, 3)
        n_core(k, 1 - c).wait_recv()
        save_g(k).start()
        normed = lambda: nbuf[k].reshape(CHUNK, width)
        first(1, normed, 0)
        second(1, 0)

        def body(r, based):
            at = (c if based else 1 - c) * side + r
            there = pl.ds(pl.multiple_of(at, STEP), STEP)
            g = gbuf[slot, there].astype(F32)
            share = stat[k, there, 0:1]
            p = pscr[there]
            pull = jnp.sum(g * p, axis=-1, keepdims=True)
            stat[k, there, 1:2] = stat[k, there, 1:2] + share * (1.0 - share) * pull
            out = share * p
            if based:
                out = out + base[ring, pl.ds(r, STEP)]
            pscr[there] = out
            grad = share * g
            nscr[there] = grad.astype(BF16)
            add_row(BOUT1, 0.25 * grad)

        over_rows(side, functools.partial(body, based=True))
        over_rows(side, functools.partial(body, based=False))

        @pl.when(k >= 2)
        def _():
            m_core(k - 2).wait_send()
            d_core(k - 2).wait_send()

        split_cols(ring)
        m_core(k).start()
        back(1, lambda: nscr[...], 0, ascr)
        split_rows(k, ring)
        save_g(k).wait()
        half_core(G, k, c).wait_send()
        d_core(k).start()
        weight_grads(lambda d: nbuf[k, :, :, d].reshape(CHUNK, 256), lambda: nscr[...], lambda f: ubuf[0, 1, :, f], lambda: ascr[...])

    def stage_pack(k, core):
        core(k).wait_recv()
        packed[k] = (mown[...] + mrecv[lax.rem(k, 4)].astype(F32)).astype(BF16)

    def group_copy(a, g):
        part = pl.ds(g * span, span)
        return pltpu.make_async_remote_copy(
            src_ref=esend.at[part],
            dst_ref=erecv.at[a, part],
            send_sem=group_sem.at[a, 0, g],
            recv_sem=group_sem.at[a, 1, g],
            device_id=(me, over_y),
            device_id_type=MESH,
        )

    def plane_copy(a, d, cc):
        target = partner(d)
        return pltpu.make_async_remote_copy(
            src_ref=eown.at[d, cc],
            dst_ref=back_rows.at[a, c, me],
            send_sem=plane_sem.at[a, 0, d, cc],
            recv_sem=plane_sem.at[a, 1, d, c],
            device_id=(target, 2 * y + cc),
            device_id_type=MESH,
        )

    def plane_landed(a, d, cc):
        source = partner(d)
        ref = back_rows.at[a, cc, source]
        return pltpu.make_async_remote_copy(
            src_ref=ref,
            dst_ref=ref,
            send_sem=plane_sem.at[a, 0, d, cc],
            recv_sem=plane_sem.at[a, 1, d, cc],
            device_id=(me, over_y),
            device_id_type=MESH,
        )

    def group_rows(g):
        low = max(0, rows - cap * blocks + cap * 4 * g * span) // CHUNK
        high = min(chunks, -(-(cap * 4 * (g + 1) * span) // CHUNK))
        return low, high

    def expand(g, a):
        low, high = group_rows(g)
        if a:
            group_copy(0, g).wait_send()
        number = lax.broadcasted_iota(jnp.int32, (2 * capp, 128), 1) + low * CHUNK

        def part(i, yy, into):
            where = packed_place(4 * (g * span + i) + 2 * yy, 2)
            hot = jnp.concatenate(
                [jnp.where(where == number + 128 * t, 1.0, 0.0).astype(BF16) for t in range((high - low) * CHUNK // 128)], axis=1
            )
            block = dot(hot, packed[low:high].reshape((high - low) * CHUNK, half))
            into[g * span + i] = block.astype(BF16).reshape(2, capp, half)

        def far(i, carry):
            part(i, 1 - y, esend)
            return carry

        def near(i, carry):
            if a:
                finish(0, g * span + i)
            part(i, y, eown)
            return carry

        lax.fori_loop(0, span, far, 0)
        group_copy(a, g).start()
        lax.fori_loop(0, span, near, 0)

    def self_copy(a):
        return pltpu.make_async_copy(eown.at[0, c], back_rows.at[a, c, me], local_sem.at[1])

    def finish(a, d):
        @pl.when(d > 0)
        def _():
            plane_copy(a, d, 0).wait_send()
            plane_copy(a, d, 1).wait_send()

        @pl.when(d == 0)
        def _():
            plane_copy(a, 0, 1 - c).wait_send()
            self_copy(a).wait()

    def give_back(a, g):
        group_copy(a, g).wait_recv()

        def one(i, carry):
            d = g * span + i
            eown[d] = (eown[d].astype(F32) + erecv[a, d].astype(F32)).astype(BF16)

            @pl.when(d > 0)
            def _():
                plane_copy(a, d, 0).start()
                plane_copy(a, d, 1).start()

            @pl.when(d == 0)
            def _():
                plane_copy(a, 0, 1 - c).start()
                self_copy(a).start()

            return carry

        lax.fori_loop(0, span, one, 0)

    ready = [group_rows(g)[1] for g in range(groups)]
    late = sorted((g for g in range(groups) if ready[g] >= chunks), key=lambda g: (1 - g % 2, g))
    order = [g for g in range(groups) if g not in late] + late

    def loop2(k, carry):
        @pl.when(k < chunks)
        def _():
            load_x(k).wait()

        @pl.when(k + 1 < chunks)
        def _():
            load_x(k + 1).start()

        @pl.when(k >= 2)
        def _():
            stage_sum(k - 2, d_core, d_y, 1)

        for i in range(1, chunks):

            @pl.when(k == i - 1)
            def _():
                fetch(G, i)

        @pl.when(k < chunks)
        def _():
            stage_c(k)

        for i in range(1, chunks):

            @pl.when(k == i - 1)
            def _():
                pack(G, i)

        @pl.when(k >= 2)
        def _():
            stage_pack(k - 2, m_core)

        for g in range(groups):
            if ready[g] < chunks:

                @pl.when(k - 1 == ready[g])
                def _():
                    expand(g, 0)

        @pl.when(jnp.logical_and(k >= 1, k <= chunks))
        def _():
            stage_d(k - 1)

        return carry

    lax.fori_loop(0, chunks + 2, loop2, 0)
    for k in (chunks - 2, chunks - 1):
        m_core(k).wait_send()
        d_core(k).wait_send()

    def save_grads(layer):
        return pltpu.make_async_copy(wbuf.at[layer], gw.at[layer], w_sem.at[layer, 0])

    def round_grads(layer, wipe):
        def body(i, carry):
            rng = pl.ds(pl.multiple_of(i * 32, 32), 32)
            wbuf[layer, 0, rng] = acc_in[rng].astype(BF16)
            wbuf[layer, 1, rng] = acc_out[rng].astype(BF16)
            if wipe:
                acc_in[rng] = jnp.zeros((32, hidden), F32)
                acc_out[rng] = jnp.zeros((32, width), F32)
            return carry

        lax.fori_loop(0, width // 32, body, 0)

    round_grads(1, True)
    save_grads(1).start()
    load_x(0).start()
    load_g(0).start()
    load_u(0).start()
    for g in late:
        expand(g, 0)
    save_grads(1).wait()

    def stage_g(k):
        ring, slot = lax.rem(k, 2), lax.rem(k, 3)
        d_y(k).wait_recv()
        n_core(k, c).wait_send()

        def body(r):
            here = pl.ds(r, STEP)
            there = pl.ds(pl.multiple_of(c * side + r, STEP), STEP)
            g = gbuf[slot, there].astype(F32)
            share = stat[k, there, 0:1]
            dn = ysend[1, k, here].astype(F32) + yrecv[1, k, here].astype(F32)
            unit = unit1[k, here].astype(F32)
            w = dn * gains[1:2]
            add_row(GAIN1, 0.5 * dn * unit)
            add_row(SHIFT1, 0.5 * dn)
            grad = share * g + stat[k, there, 2:3] * (
                w - jnp.mean(w, axis=-1, keepdims=True) - unit * jnp.mean(w * unit, axis=-1, keepdims=True)
            )
            nbuf[k, c, here] = grad.astype(BF16)
            add_row(BOUT0, 0.5 * grad)
            base[ring, here] = 0.5 * (grad + (1.0 - share) * g)

        over_rows(side, body)
        dp_core(k, c).start()

    def before_at(k):
        per = chunks // 2
        return wbuf.at[1, k // per, pl.ds(pl.multiple_of(lax.rem(k, per) * CHUNK, CHUNK), CHUNK)]

    def stage_h(k):
        ring, slot = lax.rem(k, 2), lax.rem(k, 3)
        dp_core(k, 1 - c).wait_recv()
        back(0, lambda: nbuf[k].reshape(CHUNK, width), ring, before_at(k))

        def body(r, based):
            at = (c if based else 1 - c) * side + r
            there = pl.ds(pl.multiple_of(at, STEP), STEP)
            x = xbuf[slot, there].astype(F32)
            pull = stat[k, there, 1:2]
            unit, scale = row_stats(x)
            dn = pscr[there]
            w = dn * gains[0:1]
            add_row(GAIN0, dn * unit)
            add_row(SHIFT0, dn)
            add_row(CENT, pull * x)
            out = pull * center[...] + scale * (
                w - jnp.mean(w, axis=-1, keepdims=True) - unit * jnp.mean(w * unit, axis=-1, keepdims=True)
            )
            if based:
                out = out + base[ring, pl.ds(r, STEP)]
            pscr[there] = out

        over_rows(side, functools.partial(body, based=True))
        over_rows(side, functools.partial(body, based=False))

        @pl.when(k >= 2)
        def _():
            z_core(k - 2).wait_send()

        split_cols(ring)
        z_core(k).start()

    def stage_w(k, carry):
        load_un(k).wait()

        @pl.when(k + 1 < chunks)
        def _():
            load_un(k + 1).start()

        slot = lax.rem(k, 2)
        weight_grads(
            lambda d: ubuf[slot, 2, :, d],
            lambda: nbuf[k].reshape(CHUNK, width),
            lambda f: ubuf[slot, 1, :, f],
            lambda: before_at(k)[...],
        )
        return carry

    def loop3(k, carry):
        @pl.when(k < chunks)
        def _():
            load_x(k).wait()
            load_g(k).wait()

        @pl.when(k + 1 < chunks)
        def _():
            load_x(k + 1).start()
            load_g(k + 1).start()

        @pl.when(k >= 2)
        def _():
            stage_pack(k - 2, z_core)

        @pl.when(k < chunks)
        def _():
            stage_g(k)

        @pl.when(k >= 1)
        def _():
            load_u(k - 1).wait()

        @pl.when(jnp.logical_and(k >= 1, k < chunks))
        def _():
            load_u(k).start()

        @pl.when(k >= 1)
        def _():
            stage_h(k - 1)

        for n, g in enumerate(order):

            @pl.when(k == 1 + n * chunks // groups)
            def _():
                give_back(0, g)

        for g in range(groups):
            if ready[g] < chunks:

                @pl.when(k - 1 == ready[g])
                def _():
                    expand(g, 1)

        return carry

    lax.fori_loop(0, chunks + 1, loop3, 0)
    stage_pack(chunks - 1, z_core)
    for g in late:
        expand(g, 1)
    load_un(0).start()

    for row in range(8):
        mine[row : row + 1] = jnp.sum(tally[row], axis=0, keepdims=True)
    for layer in range(SUBLAYERS):
        gb_in[layer : layer + 1] = jnp.sum(btally[layer], axis=0, keepdims=True)
    tallies[place] = mine[...]

    def tally_copy(i, to):
        return pltpu.make_async_remote_copy(
            src_ref=mine,
            dst_ref=tallies.at[place],
            send_sem=sum_sem.at[0, i],
            recv_sem=sum_sem.at[1, i],
            device_id=(me, to),
            device_id_type=MESH,
        )

    def tally_landed(i, frm):
        ref = tallies.at[frm]
        return pltpu.make_async_remote_copy(
            src_ref=ref, dst_ref=ref, send_sem=sum_sem.at[0, i], recv_sem=sum_sem.at[1, i], device_id=(me, frm), device_id_type=MESH
        )

    others = (over_c, over_y, over_both)
    for i, to in enumerate(others):
        tally_copy(i, to).start()
    for g in order[: groups - len(late)]:
        give_back(1, g)
    lax.fori_loop(0, chunks // 2, stage_w, 0)
    give_back(1, late[0])
    lax.fori_loop(chunks // 2, chunks, stage_w, 0)
    give_back(1, late[1])
    round_grads(0, False)
    save_grads(0).start()
    for g in late[2:]:
        give_back(1, g)

    def gather_back(a, result):
        def wait(d, carry):
            for cc in range(2):

                @pl.when(jnp.logical_or(d > 0, cc != c))
                def _():
                    plane_landed(a, d, cc).wait_recv()

            return carry

        lax.fori_loop(0, experts, wait, 0)
        if a:
            self_copy(1).wait()
        lane = lax.broadcasted_iota(jnp.int32, (experts * capp, 128), 1)
        where = slots[...].reshape(experts * capp, 128)
        for j in range(2):
            copy = pltpu.make_async_copy(back_rows.at[a, j], window.at[pl.ds(0, experts)], local_sem.at[0])
            copy.start()
            copy.wait()
            for i, hold in enumerate((nscr, ascr)):
                hot = jnp.concatenate(
                    [jnp.where(where == lane + (i * CHUNK + 128 * t), 1.0, 0.0).astype(BF16) for t in range(CHUNK // 128)], axis=1
                )
                block = window[:experts]
                hold[:, j * half : (j + 1) * half] = dot_tn(hot, block.reshape(experts * capp, half)).astype(BF16)
        for i, hold in enumerate((nscr, ascr)):
            pltpu.make_async_copy(hold, result.at[pl.ds(i * CHUNK, CHUNK)], local_sem.at[2 + i]).start()

    def gathered(result):
        for i, hold in enumerate((nscr, ascr)):
            pltpu.make_async_copy(hold, result.at[pl.ds(i * CHUNK, CHUNK)], local_sem.at[2 + i]).wait()

    gather_back(0, mixed)
    for i, frm in enumerate(others):
        tally_landed(i, frm).wait_recv()
        tally_copy(i, frm).wait_send()
    sums[...] = (tallies[0] + tallies[1]) + (tallies[2] + tallies[3])
    gathered(mixed)
    gather_back(1, gtok)
    for g in range(groups):
        group_copy(1, g).wait_send()

    def last(d, carry):
        @pl.when(d > 0)
        def _():
            plane_copy(1, d, 0).wait_send()
            plane_copy(1, d, 1).wait_send()

        @pl.when(d == 0)
        def _():
            plane_copy(1, 0, 1 - c).wait_send()

        return carry

    lax.fori_loop(0, experts, last, 0)

    over_peers(lambda i, cc: plane(COUNT, i, cc).wait_send())
    for a in (X, G):
        over_peers(lambda i, cc: forward(a, i, cc).wait_send())

    def last_chunk(k, carry):
        p_y(k).wait_send()
        d_y(k).wait_send()
        dp_core(k, c).wait_send()
        return carry

    lax.fori_loop(0, chunks, last_chunk, 0)
    for k in (chunks - 2, chunks - 1):
        z_core(k).wait_send()
    save_grads(0).wait()
    gathered(gtok)


def finish_kernel(
    mixed, gtok, gw, gb_in, sums, mixed_out, gtok_out, gw_in, gw_out, gb_in_out, gain, shift, b_out, center,
    narrow, wide, tok_narrow, tok_wide, mix, in_sem, out_sem, tok_sem,
):
    width = gw.shape[2]
    per = width // CHUNK

    def spot(n):
        return n // (2 * per), n // per % 2, pl.ds(n % per * CHUNK, CHUNK)

    def load(n):
        layer, which, part = spot(n)
        return pltpu.make_async_copy(gw.at[layer, which, part], narrow.at[n], in_sem.at[n])

    def store(n):
        layer, which, part = spot(n)
        return pltpu.make_async_copy(wide.at[n], (gw_in, gw_out)[which].at[layer, part], out_sem.at[n])

    pieces = 2 * SUBLAYERS * per
    for n in range(pieces):
        load(n).start()
    tok_load = pltpu.make_async_copy(gtok, tok_narrow, tok_sem.at[0])
    tok_store = pltpu.make_async_copy(tok_wide, gtok_out, tok_sem.at[1])
    mix_load = pltpu.make_async_copy(mixed, mix, tok_sem.at[2])
    mix_store = pltpu.make_async_copy(mix, mixed_out, tok_sem.at[3])
    tok_load.start()
    mix_load.start()
    for n in range(pieces):
        load(n).wait()
        wide[n] = narrow[n].astype(F32)
        store(n).start()
    mix_load.wait()
    mix_store.start()
    tok_load.wait()
    tok_wide[...] = tok_narrow[...].astype(F32)
    tok_store.start()
    gb_in_out[...] = gb_in[...]
    gain[...] = sums[0:2]
    shift[...] = sums[2:4]
    b_out[...] = sums[4:6]
    center[...] = sums[6:7]
    for n in range(pieces):
        store(n).wait()
    tok_store.wait()
    mix_store.wait()


def finish(mixed, gtok, gw, gb_in, sums):
    toks, width = mixed.shape
    pieces = 2 * SUBLAYERS * width // CHUNK
    vmem = pl.BlockSpec(memory_space=pltpu.VMEM)
    hbm = pl.BlockSpec(memory_space=pl.ANY)
    dma = pltpu.SemaphoreType.DMA

    def shape(*dims):
        return jax.ShapeDtypeStruct(dims, F32)

    return pl.pallas_call(
        finish_kernel,
        out_shape=(
            jax.ShapeDtypeStruct((toks, width), BF16),
            shape(toks, width),
            shape(SUBLAYERS, width, width),
            shape(SUBLAYERS, width, width),
            shape(SUBLAYERS, width),
            shape(SUBLAYERS, width),
            shape(SUBLAYERS, width),
            shape(SUBLAYERS, width),
            shape(1, width),
        ),
        in_specs=[hbm, hbm, hbm, vmem, vmem],
        out_specs=(hbm, hbm, hbm, hbm, vmem, vmem, vmem, vmem, vmem),
        scratch_shapes=[
            pltpu.VMEM((pieces, CHUNK, width), BF16),
            pltpu.VMEM((pieces, CHUNK, width), F32),
            pltpu.VMEM((toks, width), BF16),
            pltpu.VMEM((toks, width), F32),
            pltpu.VMEM((toks, width), BF16),
            dma((pieces,)),
            dma((pieces,)),
            dma((4,)),
        ],
        compiler_params=pltpu.CompilerParams(vmem_limit_bytes=61 * 2**20),
        name="finish",
    )(mixed, gtok, gw, gb_in, sums)


def layers(cap, slots, tok, cot, w_in, w_out, b_in, b_out, gains, shifts, center):
    experts, capp = slots.shape[:2]
    blocks = 4 * experts
    toks, width = tok.shape
    rows = 4 * toks
    hidden = b_in.shape[1]
    half, side, chunks = width // 2, CHUNK // 2, rows // CHUNK
    span = experts // GROUPS
    windows = [row_window(k, blocks, cap, rows) for k in range(chunks)]
    reach = max(high - low for low, high in windows)
    vmem = pl.BlockSpec(memory_space=pltpu.VMEM)
    hbm = pl.BlockSpec(memory_space=pl.ANY)
    dma = pltpu.SemaphoreType.DMA
    return pl.pallas_call(
        functools.partial(layers_kernel, experts, cap),
        out_shape=(
            jax.ShapeDtypeStruct((toks, width), BF16),
            jax.ShapeDtypeStruct((toks, width), BF16),
            jax.ShapeDtypeStruct((SUBLAYERS, 2, width, width), BF16),
            jax.ShapeDtypeStruct((SUBLAYERS, hidden), F32),
            jax.ShapeDtypeStruct((8, width), F32),
            jax.ShapeDtypeStruct((chunks, 3, CHUNK, hidden), BF16),
            jax.ShapeDtypeStruct((2, 2, experts, capp, half), BF16),
            jax.ShapeDtypeStruct((2, blocks, capp, half), BF16),
            jax.ShapeDtypeStruct((rows, width), BF16),
            jax.ShapeDtypeStruct((rows, width), BF16),
        ),
        in_specs=[vmem, hbm, hbm, hbm, hbm, vmem, vmem, vmem, vmem, vmem],
        out_specs=(hbm, hbm, hbm, vmem, vmem, hbm, hbm, hbm, hbm, hbm),
        scratch_shapes=[
            pltpu.VMEM((SUBLAYERS, 2, width, width), BF16),
            pltpu.VMEM((width, hidden), F32),
            pltpu.VMEM((hidden, width), F32),
            pltpu.VMEM((3, CHUNK, width), BF16),
            pltpu.VMEM((3, CHUNK, width), BF16),
            pltpu.VMEM((reach, capp, half), BF16),
            pltpu.VMEM((blocks, 128), jnp.int32),
            pltpu.VMEM((blocks, 128), jnp.int32),
            pltpu.VMEM((experts, 16, 128), BF16),
            pltpu.VMEM((2, 3, CHUNK, hidden), BF16),
            pltpu.VMEM((chunks, 2, side, width), BF16),
            pltpu.VMEM((CHUNK, width), BF16),
            pltpu.VMEM((CHUNK, hidden), BF16),
            pltpu.VMEM((CHUNK, width), F32),
            pltpu.VMEM((2, side, width), F32),
            pltpu.VMEM((2, side, width), BF16),
            pltpu.VMEM((4, side, width), BF16),
            pltpu.VMEM((2, chunks, side, width), BF16),
            pltpu.VMEM((2, chunks, side, width), BF16),
            pltpu.VMEM((chunks, side, width), BF16),
            pltpu.VMEM((2, side, width), F32),
            pltpu.VMEM((chunks, CHUNK, 128), F32),
            pltpu.VMEM((CHUNK, half), F32),
            pltpu.VMEM((2, CHUNK, half), BF16),
            pltpu.VMEM((4, CHUNK, half), BF16),
            pltpu.VMEM((chunks, CHUNK, half), BF16),
            pltpu.VMEM((experts, 2, capp, half), BF16),
            pltpu.VMEM((experts, 2, capp, half), BF16),
            pltpu.VMEM((2, experts, 2, capp, half), BF16),
            pltpu.VMEM((8, 8, width), F32),
            pltpu.VMEM((SUBLAYERS, 8, hidden), F32),
            pltpu.VMEM((8, width), F32),
            pltpu.VMEM((4, 8, width), F32),
            dma((8, 2, chunks)),
            dma((2, 2, GROUPS)),
            dma((2, 2, experts, 2)),
            dma((2, 3)),
            dma((SUBLAYERS, 2)),
            dma((3,)),
            dma((3,)),
            dma((2, 2)),
            dma((4,)),
            dma((3, 4, experts, 2)),
            dma((2, 2, chunks)),
        ],
        compiler_params=pltpu.CompilerParams(collective_id=0, has_side_effects=True, vmem_limit_bytes=62 * 2**20),
        name="layers",
    )(slots, tok, cot, w_in, w_out, b_in, b_out, gains, shifts, center)


def on_device(experts, places, tokens, dispatch_rows, w_in, w_out, b_in, b_out, ln_gain, ln_bias, centroid, cotangent):
    slots = dispatch_rows[0]
    toks = tokens.shape[0]
    cap = slots.shape[1]
    capp = -(-cap // 16) * 16
    padded = jnp.pad(slots, ((0, 0), (0, capp - cap)), constant_values=toks)
    spread = jnp.broadcast_to(padded[:, :, None], (experts, capp, 128))
    parts = layers(cap, spread, tokens, cotangent, w_in[0], w_out[0], b_in[0], b_out[0], ln_gain[0], ln_bias[0], centroid)
    mixed, gtok, gw_in, gw_out, gb_in, gain, shift, bias, center = finish(*parts[:5])
    return mixed, gtok, gw_in[None], gw_out[None], gb_in[None], bias[None], gain[None], shift[None], center


def solution(mesh):
    rows = P(("expert", "hidden"), None)
    return jax.shard_map(
        functools.partial(on_device, mesh.shape["expert"], mesh.shape["hidden"]),
        mesh=mesh,
        in_specs=(
            rows,
            P(("expert", "hidden"), None, None),
            P("expert", None, None, "hidden"),
            P("expert", None, "hidden", None),
            P("expert", None, "hidden"),
            P("expert", None, None),
            P("expert", None, None),
            P("expert", None, None),
            P("expert", None),
            rows,
        ),
        out_specs=(
            rows,
            rows,
            P("expert", None, None, "hidden"),
            P("expert", None, "hidden", None),
            P("expert", None, "hidden"),
            P("expert", None, None),
            P("expert", None, None),
            P("expert", None, None),
            P("expert", None),
        ),
        check_vma=False,
    )
```
